256 devices in a mesh: loop: 16 (over y_hi, z), grp: 16 (over y_lo, x, core).
Axes of the slice: x: 4, y: 4 (y_hi: 2, y_lo: 2; y = y_hi * 2 + y_lo), z: 8, core: 2. Of those that a mesh axis runs over, the one named last changes fastest.
Arguments:
- queries: bfloat16 [24576, 1024], P(('loop', 'grp')), may hold values from -3 to 3
- passages: bfloat16 [24576, 1024], P(('grp', 'loop')), may hold values from -3 to 3
- pair: int32 [24576], P(('loop', 'grp')), may hold values from 0 to 24575, each once
Outputs:
- query_grad: bfloat16 [24576, 1024], P(('loop', 'grp'))
- passage_grad: bfloat16 [24576, 1024], P(('grp', 'loop'))
- loss: float32 [], replicated
The draws below stay inside these ranges and needn't reach their ends.
Inputs may be any that keep to these rules, and one draw needn't show every extreme that they name: `pair`: every passage is the positive of exactly one query.
All inputs are finite; a program needn't handle non-finite values.
Results may differ from the reference program's by a relative error of at most 0.0031.
Values may be sent and summed in bfloat16 or wider, within the bound.
A program may use at most 64 MiB of HBM per device.

```python
import jax
import jax.numpy as jnp
from jax import lax

D = 1024
PAIRS = 24576


def rising_scale(count):
    steps = jnp.arange(count).astype(jnp.float32) / max(count - 1, 1)
    return jnp.exp(jnp.log(3.0) * steps)


def draw_queries(key, part):
    key = jax.random.fold_in(key, 5)
    values = jnp.clip(jax.random.normal(key, (PAIRS, D), jnp.float32), -6.0, 6.0)
    values = values * rising_scale(PAIRS)[:, None] / jnp.sqrt(jnp.float32(D))
    return values.astype(jnp.bfloat16)


def draw_passages(key, part):
    key = jax.random.fold_in(key, 6)
    values = jnp.clip(jax.random.normal(key, (PAIRS, D), jnp.float32), -6.0, 6.0)
    values = values * rising_scale(PAIRS)[:, None] / jnp.sqrt(jnp.float32(D))
    return values.astype(jnp.bfloat16)


def setup_inputs(seed: int = 0) -> dict:
    streams_of = jax.random.split(jax.random.key(seed), 4)
    queries = draw_queries(jax.random.fold_in(streams_of[3], 71), 0)
    passages = draw_passages(jax.random.fold_in(streams_of[3], 71), 0)
    pair = jax.random.permutation(streams_of[2], PAIRS).astype(jnp.int32)
    return dict(queries=queries, passages=passages, pair=pair)


inv_temp = 50.0
grad_scale = 25.0


def tile_scores(block, passages):
    return lax.dot_general(block, passages, (((1,), (1,)), ((), ())), preferred_element_type=jnp.float32) * inv_temp


def reference(queries, passages, pair):
    blocks = max(1, PAIRS // 512)
    height = PAIRS // blocks
    query_blocks = queries.reshape(blocks, height, D)
    pair_blocks = pair.reshape(blocks, height)
    columns = jnp.arange(PAIRS, dtype=jnp.int32)

    def first(carry, block):
        col_peak, col_sum = carry
        scores = tile_scores(block, passages)
        row_peak = jnp.max(scores, axis=1)
        row_lse = row_peak + jnp.log(jnp.sum(jnp.exp(scores - row_peak[:, None]), axis=1))
        fresh = jnp.maximum(col_peak, jnp.max(scores, axis=0))
        col_sum = col_sum * jnp.exp(col_peak - fresh) + jnp.sum(jnp.exp(scores - fresh[None, :]), axis=0)
        return (fresh, col_sum), row_lse

    start = (jnp.full((PAIRS,), -jnp.inf, jnp.float32), jnp.zeros((PAIRS,), jnp.float32))
    (col_peak, col_sum), row_lse = lax.scan(first, start, query_blocks)
    col_lse = col_peak + jnp.log(col_sum)

    def second(total, item):
        block, targets, lse_block = item
        scores = tile_scores(block, passages)
        hit = targets[:, None] == columns[None, :]
        weights = (jnp.exp(scores - lse_block[:, None]) + jnp.exp(scores - col_lse[None, :])
                   - 2.0 * hit.astype(jnp.float32)).astype(jnp.bfloat16)
        query_part = (jnp.dot(weights, passages, preferred_element_type=jnp.float32) * grad_scale).astype(jnp.bfloat16)
        total = total + lax.dot_general(weights, block, (((0,), (0,)), ((), ())), preferred_element_type=jnp.float32)
        positive = jnp.sum(jnp.where(hit, scores, jnp.float32(0.0)))
        return total, (query_part, positive)

    total, (query_parts, positives) = lax.scan(second, jnp.zeros((PAIRS, D), jnp.float32), (query_blocks, pair_blocks, row_lse))
    loss = (jnp.sum(row_lse) + jnp.sum(col_lse) - 2.0 * jnp.sum(positives)) / (2.0 * PAIRS)
    query_grad = query_parts.reshape(PAIRS, D)
    passage_grad = (total * grad_scale).astype(jnp.bfloat16)
    return query_grad, passage_grad, loss
```

```python
import functools
import math

import jax
import jax.numpy as jnp
from jax import lax
from jax.experimental import pallas as pl
from jax.experimental.pallas import tpu as pltpu
from jax.sharding import PartitionSpec as P

MESH = pl.DeviceIdType.MESH
D = 1024
OWN = 96
HALF = 48
ROWS = 1536
BUNDLE = 192
CHUNK = 384
COLS = 512
PAIRS = 24576
TO_LOG2 = 50.0 * math.log2(math.e)
LN2 = math.log(2.0)
GRAD_SCALE = 25.0
LEVELS = 32000.0
SMALLEST = 1e-30
LOWEST = -1e38
RING4 = (0, 1, -1, 2)
RING8 = (0, 1, -1, 2, -2, 3, -3, 4)
AT4 = {0: 0, 1: 1, -1: 2, 2: 3}
AT8 = {0: 0, 1: 1, -1: 2, 2: 3, -2: 4, 3: 5, -3: 6, 4: 7}
MESSAGES = 136
f32 = jnp.float32
bf16 = jnp.bfloat16
i16 = jnp.int16


def tiles(rows, cols):
    return (rows // 16) * (cols // 128) + 1


def kernel(
    q_in, p_in, pair_in, qg_out, pg_out, loss_out,
    q_all, p_all, scores, w, wt,
    row_peak, row_sum, col_peak, col_sum,
    row_stats, col_stats, row_lse, row_rep, pair_rep, order, col_lse, col_rep, col_index,
    term, sib, ab_far_out, ab_far_in, ab_near_out, ab_near_in,
    ab2_far_out, ab2_far_in, ab2_near_out, ab2_near_in,
    z_far_out, z_far_in, z_out, z_in, loss_out_buf, loss_in_buf, positive,
    send_sem, recv_sem,
):
    loop = lax.axis_index("loop")
    grp = lax.axis_index("grp")
    core = lax.rem(grp, 2)
    x = lax.rem(lax.div(grp, 2), 4)
    y = lax.div(loop, 8) * 2 + lax.div(grp, 8)
    z = lax.rem(loop, 8)

    def device(dx=0, dy=0, dz=0, dc=0):
        x2, y2 = lax.rem(x + dx + 4, 4), lax.rem(y + dy + 4, 4)
        z2, c2 = lax.rem(z + dz + 8, 8), lax.rem(core + dc, 2)
        return {
            "loop": lax.div(y2, 2) * 8 + z2,
            "grp": (lax.rem(y2, 2) * 4 + x2) * 2 + c2,
        }

    plane = [(dx, dy) for dx in range(4) for dy in range(4) if dx or dy]
    column = [(dz, dc) for dz in range(8) for dc in range(2) if dz or dc]

    barrier = pltpu.get_barrier_semaphore()
    for dx, dy in plane:
        pl.semaphore_signal(barrier, inc=1, device_id=device(dx=dx, dy=dy), device_id_type=MESH)
    for dz, dc in column:
        pl.semaphore_signal(barrier, inc=1, device_id=device(dz=dz, dc=dc), device_id_type=MESH)

    count = [0]
    sent = []

    def send(src, dst, **where):
        k = count[0]
        count[0] += 1
        copy = pltpu.make_async_remote_copy(
            src_ref=src, dst_ref=dst, send_sem=send_sem.at[k], recv_sem=recv_sem.at[k],
            device_id=device(**where), device_id_type=MESH,
        )
        copy.start()
        sent.append(copy)
        return copy

    def q_at(half, p, q, cols=(0, D)):
        return q_all.at[pl.ds((2 * p + half) * BUNDLE + q * HALF, HALF), pl.ds(*cols)]

    def p_at(pos, rel, h=None):
        start = pos * BUNDLE + rel * OWN
        if h is None:
            return p_all.at[pl.ds(start, OWN), :]
        return p_all.at[pl.ds(start + h * HALF, HALF), :]

    q_all[pl.ds(0, HALF), :] = q_in[pl.ds(0, HALF), :]
    q_all[pl.ds(BUNDLE, HALF), :] = q_in[pl.ds(HALF, HALF), :]
    p_all[pl.ds(0, OWN), :] = p_in[...]
    row_peak[...] = jnp.full(row_peak.shape, LOWEST, f32)
    row_sum[...] = jnp.zeros(row_sum.shape, f32)
    col_peak[...] = jnp.full(col_peak.shape, LOWEST, f32)
    col_sum[...] = jnp.zeros(col_sum.shape, f32)
    slot = x * 4 + y
    col_slot = z * 2 + core
    row_stats[slot] = jnp.zeros((40, 128), f32)
    col_stats[col_slot] = jnp.zeros((16, 128), f32)
    row_stats[slot, pl.ds(32, 1), pl.ds(0, OWN)] = pair_in[...].astype(f32)

    pl.semaphore_wait(barrier, len(plane) + len(column))

    first_axis, second_axis = ("dx", "dy"), ("dy", "dx")
    zs = {}
    for sign in (1, -1):
        for h in (0, 1):
            zs[sign, 1, h] = send(p_at(0, 0, h), p_at(AT8[-sign], 0, h), dz=sign)
    near1, far1, near2, far2 = {}, {}, {}, {}
    for sign in (1, -1):
        for half in (0, 1):
            near1[half, sign] = send(q_at(half, 0, 0), q_at(half, 0, AT4[-sign]), **{first_axis[half]: sign})
    sibling = {0: send(p_at(0, 0), p_at(0, 1), dc=1)}

    def spread(half, q):
        for sign in (1, -1):
            near2[half, sign, q] = send(
                q_at(half, 0, q), q_at(half, AT4[-sign], q), **{second_axis[half]: sign}
            )

    for half in (0, 1):
        spread(half, 0)
    for half in (0, 1):
        for sign in (1, -1):
            q = AT4[-sign]
            near1[half, sign].wait_recv()
            cols = (0, D // 2) if sign == 1 else (D // 2, D // 2)
            far1[half, sign] = send(q_at(half, 0, q, cols), q_at(half, 0, 3, cols), **{first_axis[half]: sign})
            spread(half, q)

    def hop(k):
        for h in (0, 1):
            for sign in (1, -1):
                if k == 4 and h != (0 if sign == 1 else 1):
                    continue
                zs[sign, k, h].wait_recv()
                if k < 3 or (k == 3 and h == (0 if sign == 1 else 1)):
                    pos, to = AT8[-sign * k], AT8[-sign * (k + 1) if k < 3 else 4]
                    zs[sign, k + 1, h] = send(p_at(pos, 0, h), p_at(to, 0, h), dz=sign)
        for pos in (AT8[k], AT8[-k]) if k < 4 else (7,):
            sibling[pos] = send(p_at(pos, 0), p_at(pos, 1), dc=1)

    hop(1)
    for half in (0, 1):
        for sign in (1, -1):
            far1[half, sign].wait_recv()
        spread(half, 3)

    def block(p, k):
        rows = pl.ds(pl.multiple_of(p * CHUNK, CHUNK), CHUNK)
        cols = pl.ds(pl.multiple_of(k * COLS, COLS), COLS)
        s = lax.dot_general(
            q_all[rows, :], p_all[cols, :], (((1,), (1,)), ((), ())), preferred_element_type=f32
        ) * TO_LOG2
        scores[rows, cols] = s
        parts = [s[:, 128 * i : 128 * (i + 1)] for i in range(COLS // 128)]
        old = row_peak[rows, :]
        peak = functools.reduce(jnp.maximum, parts, old)
        total = row_sum[rows, :] * jnp.exp2(old - peak)
        for part in parts:
            total += jnp.exp2(part - peak)
        row_peak[rows, :] = peak
        row_sum[rows, :] = total
        s3 = s.reshape(CHUNK // 8, 8, COLS)
        old = col_peak[:, cols]
        peak = jnp.maximum(old, jnp.max(s3, axis=0))
        col_sum[:, cols] = col_sum[:, cols] * jnp.exp2(old - peak) + jnp.sum(jnp.exp2(s3 - peak[None]), axis=0)
        col_peak[:, cols] = peak

    def blocks(start, stop, k):
        def body(p, _):
            block(p, k)
            return 0

        lax.fori_loop(start, stop, body, 0)

    for pos in (0, 1, 2):
        sibling[pos].wait_recv()
    block(0, 0)
    hop(2)
    for q in range(4):
        for half in (0, 1):
            for sign in (1, -1):
                near2[half, sign, q].wait_recv()
                if (q < 2) == (sign == 1):
                    far2[half, q] = send(
                        q_at(half, AT4[-sign], q), q_at(half, 3, q), **{second_axis[half]: sign}
                    )
    blocks(1, 3, 0)
    hop(3)
    for pos in (3, 4, 5, 6):
        sibling[pos].wait_recv()
    blocks(0, 3, 1)
    hop(4)
    for half in (0, 1):
        for q in range(4):
            far2[half, q].wait_recv()

    def last(k, _):
        block(3, k)
        return 0

    lax.fori_loop(0, 2, last, 0)
    sibling[7].wait_recv()
    blocks(0, 4, 2)

    def piece(half, p, q):
        dx, dy = (RING4[q], RING4[p]) if half == 0 else (RING4[p], RING4[q])
        return lax.rem(x + dx + 4, 4) * 4 + lax.rem(y + dy + 4, 4)

    for b in range(8):
        p, half = b // 2, b % 2
        rows = pl.ds(b * BUNDLE, BUNDLE)
        lanes = row_peak[rows, :]
        peak = jnp.max(lanes, axis=1, keepdims=True)
        total = jnp.sum(row_sum[rows, :] * jnp.exp2(lanes - peak), axis=1, keepdims=True)
        lse = jnp.broadcast_to(peak + jnp.log(total) * (1.0 / LN2), (BUNDLE, 128)).T
        for q in range(4):
            row_stats[slot, pl.ds(half * 16 + piece(half, p, q), 1), pl.ds(0, HALF)] = lse[
                0:1, q * HALF : (q + 1) * HALF
            ]
    row_msgs = [send(row_stats.at[slot], row_stats.at[slot], dx=dx, dy=dy) for dx, dy in plane]

    def owner(pos, rel):
        return lax.rem(z + RING8[pos] + 8, 8) * 2 + lax.rem(core + rel, 2)

    peak = jnp.max(col_peak[...], axis=0, keepdims=True)
    total = jnp.sum(col_sum[...] * jnp.exp2(col_peak[...] - peak), axis=0, keepdims=True)
    lse = peak + jnp.log(total) * (1.0 / LN2)
    for pos in range(8):
        for rel in (0, 1):
            start = pos * BUNDLE + rel * OWN
            col_stats[col_slot, pl.ds(owner(pos, rel), 1), pl.ds(0, OWN)] = lse[:, start : start + OWN]
    col_msgs = [send(col_stats.at[col_slot], col_stats.at[col_slot], dz=dz, dc=dc) for dz, dc in column]

    j = lax.broadcasted_iota(jnp.int32, (1, ROWS), 1)
    part = lax.shift_right_logical(j * 683, 16)
    within = j - part * OWN
    pos = lax.shift_right_logical(part, 1)
    away = lax.shift_right_logical(pos + 1, 1)
    away = jnp.where((pos & 1) == 1, away, -away)
    z2 = (z + away + 8) & 7
    c2 = (core + part) & 1
    first = (lax.div(grp, 2) * 2 + c2) * 16 + lax.div(loop, 8) * 8 + z2
    col_index[...] = (first * OWN + within).astype(f32)

    for m in row_msgs:
        m.wait_recv()
    stats = row_stats[:, 0:32, :]
    peak = jnp.max(stats, axis=0)
    lse = peak + jnp.log(jnp.sum(jnp.exp2(stats - peak[None]), axis=0)) * (1.0 / LN2)
    row_lse[...] = lse
    lane = lax.broadcasted_iota(jnp.int32, (32, 128), 1)
    share = jnp.sum(jnp.where(lane < HALF, lse, 0.0).reshape(4, 8, 128), axis=0)
    order[pl.ds(64, 64), :] = jnp.zeros((64, 128), f32)
    for b in range(8):
        p, half = b // 2, b % 2
        for q in range(4):
            at = piece(half, p, q)
            order[pl.ds(4 * b + q, 1), :] = row_lse[pl.ds(half * 16 + at, 1), :]
            order[pl.ds(32 + 4 * b + q, 1), :] = row_stats[at, pl.ds(32, 1), :]
    turned = order[...].T
    for b in range(8):
        half = b % 2
        for q in range(4):
            n = 4 * b + q
            rows = pl.ds(n * HALF, HALF)
            row_rep[rows, :] = jnp.broadcast_to(turned[0:HALF, n : n + 1], (HALF, 128))
            pair_rep[rows, :] = jnp.broadcast_to(
                turned[half * HALF : (half + 1) * HALF, 32 + n : 33 + n], (HALF, 128)
            )

    for m in col_msgs:
        m.wait_recv()
    stats = col_stats[...]
    peak = jnp.max(stats, axis=0)
    lse = peak + jnp.log(jnp.sum(jnp.exp2(stats - peak[None]), axis=0)) * (1.0 / LN2)
    col_lse[...] = lse
    lane = lax.broadcasted_iota(jnp.int32, (16, 128), 1)
    share = share + jnp.sum(jnp.where(lane < OWN, lse, 0.0).reshape(2, 8, 128), axis=0)
    col_rep[...] = jnp.concatenate(
        [col_lse[pl.ds(owner(pos, rel), 1), :][:, 0:OWN] for pos in range(8) for rel in (0, 1)], axis=1
    )

    positive[...] = jnp.zeros((8, 128), f32)

    def weigh(p):
        rows = pl.ds(p * CHUNK, CHUNK)

        def body(n, _):
            cols = pl.ds(pl.multiple_of(n * 128, 128), 128)
            s = scores[rows, cols]
            hit = pair_rep[rows, :] == col_index[:, cols]
            weight = jnp.exp2(s - row_rep[rows, :]) + jnp.exp2(s - col_rep[:, cols]) - jnp.where(hit, 2.0, 0.0)
            positive[...] += jnp.sum(jnp.where(hit, s, 0.0).reshape(CHUNK // 8, 8, 128), axis=0)
            rounded = weight.astype(bf16)
            w[rows, cols] = rounded
            wt[cols, rows] = rounded.T
            return 0

        lax.fori_loop(0, ROWS // 128, body, 0)

    def query_term(b):
        rows = pl.ds(b * BUNDLE, BUNDLE)

        def body(n, _):
            cols = pl.ds(pl.multiple_of(n * 256, 256), 256)
            scores[rows, cols] = jnp.dot(w[rows, :], p_all[:, cols], preferred_element_type=f32)
            return 0

        lax.fori_loop(0, D // 256, body, 0)

    sib_msgs = {}

    def passage_term(pos):
        rows = pl.ds(pos * BUNDLE, BUNDLE)

        def body(n, _):
            cols = pl.ds(pl.multiple_of(n * 256, 256), 256)
            term[rows, cols] = jnp.dot(wt[rows, :], q_all[:, cols], preferred_element_type=f32)
            return 0

        lax.fori_loop(0, D // 256, body, 0)
        sib_msgs[pos] = send(term.at[pl.ds(pos * BUNDLE + OWN, OWN), :], sib.at[pl.ds(pos * OWN, OWN), :], dc=1)

    def add_sibling(pos):
        sib_msgs[pos].wait_recv()
        term[pl.ds(pos * BUNDLE, OWN), :] += sib[pl.ds(pos * OWN, OWN), :]

    def encode(ref, r0, rows, c0, cols, buf):
        peak = functools.reduce(
            jnp.maximum,
            [
                jnp.max(jnp.abs(ref[pl.ds(r0, rows), pl.ds(c0 + 128 * i, 128)]).reshape(rows // 8, 8, 128), axis=0)
                for i in range(cols // 128)
            ],
        )
        power = jnp.floor(jnp.log(jnp.maximum(peak, SMALLEST)) * (1.0 / LN2)) + 1.0
        factor = (jnp.exp2(-power) * LEVELS)[None]
        n = rows // 16
        for i in range(cols // 128):
            v = ref[pl.ds(r0, rows), pl.ds(c0 + 128 * i, 128)].reshape(rows // 8, 8, 128) * factor
            buf[pl.ds(i * n, n)] = jnp.round(v).astype(jnp.int32).reshape(n, 16, 128).astype(i16)
        both = jnp.concatenate([power, power], axis=0).astype(jnp.int32)
        buf[pl.ds(n * (cols // 128), 1)] = both.astype(i16)[None]

    def add_decoded(ref, r0, rows, c0, cols, buf):
        n = rows // 16
        power = buf[n * (cols // 128)].astype(jnp.int32).astype(f32)[0:8]
        factor = (jnp.exp2(power) * (1.0 / LEVELS))[None]
        for i in range(cols // 128):
            v = buf[pl.ds(i * n, n)].astype(jnp.int32).astype(f32).reshape(rows // 8, 8, 128) * factor
            ref[pl.ds(r0, rows), pl.ds(c0 + 128 * i, 128)] += v.reshape(rows, 128)

    msgs = {}

    def far_stage(half):
        b = 3 * 2 + half
        query_term(b)
        for sign, s in ((1, 0), (-1, 1)):
            encode(scores, b * BUNDLE + s * OWN, OWN, 0, D, ab_far_out.at[half, s])
            msgs["far", half, s] = send(
                ab_far_out.at[half, s], ab_far_in.at[half, s], **{second_axis[half]: sign}
            )

    def near_term(half, s):
        query_term((1 + s) * 2 + half)

    def near_send(half, s, sign):
        b = (1 + s) * 2 + half
        msgs["far", half, s].wait_recv()
        add_decoded(scores, b * BUNDLE + s * OWN, OWN, 0, D, ab_far_in.at[half, s])
        encode(scores, b * BUNDLE, BUNDLE, 0, D, ab_near_out.at[half, s])
        msgs["near", half, s] = send(ab_near_out.at[half, s], ab_near_in.at[half, s], **{second_axis[half]: sign})

    def own_stage(half):
        for s in (0, 1):
            msgs["near", half, s].wait_recv()
            add_decoded(scores, half * BUNDLE, BUNDLE, 0, D, ab_near_in.at[half, s])
        for sign, s in ((1, 0), (-1, 1)):
            encode(scores, half * BUNDLE + 3 * HALF, HALF, s * (D // 2), D // 2, ab2_far_out.at[half, s])
            msgs["far2", half, s] = send(ab2_far_out.at[half, s], ab2_far_in.at[half, s], **{first_axis[half]: sign})

    def near2_stage(half):
        for sign, s in ((1, 0), (-1, 1)):
            row = half * BUNDLE + (1 + s) * HALF
            msgs["far2", half, s].wait_recv()
            add_decoded(scores, row, HALF, s * (D // 2), D // 2, ab2_far_in.at[half, s])
            encode(scores, row, HALF, 0, D, ab2_near_out.at[half, s])
            msgs["near2", half, s] = send(
                ab2_near_out.at[half, s], ab2_near_in.at[half, s], **{first_axis[half]: sign}
            )

    def query_out(half):
        row = half * BUNDLE
        for s in (0, 1):
            msgs["near2", half, s].wait_recv()
            add_decoded(scores, row, HALF, 0, D, ab2_near_in.at[half, s])
        qg_out[pl.ds(half * HALF, HALF), :] = (scores[pl.ds(row, HALF), pl.ds(0, D)] * GRAD_SCALE).astype(bf16)

    def z_far():
        add_sibling(7)
        for sign, s in ((1, 0), (-1, 1)):
            encode(term, 7 * BUNDLE + s * HALF, HALF, 0, D, z_far_out.at[s])
            msgs["z", 4, s] = send(z_far_out.at[s], z_far_in.at[s], dz=sign)

    def z_near(k):
        for sign, s in ((1, 0), (-1, 1)):
            pos = AT8[sign * k]
            add_sibling(pos)
            msgs["z", k + 1, s].wait_recv()
            if k == 3:
                add_decoded(term, pos * BUNDLE + s * HALF, HALF, 0, D, z_far_in.at[s])
            else:
                add_decoded(term, pos * BUNDLE, OWN, 0, D, z_in.at[k, s])
            encode(term, pos * BUNDLE, OWN, 0, D, z_out.at[k - 1, s])
            msgs["z", k, s] = send(z_out.at[k - 1, s], z_in.at[k - 1, s], dz=sign)

    def passage_out():
        add_sibling(0)
        for s in (0, 1):
            msgs["z", 1, s].wait_recv()
            add_decoded(term, 0, OWN, 0, D, z_in.at[0, s])
        pg_out[...] = (term[pl.ds(0, OWN), :] * GRAD_SCALE).astype(bf16)

    loss_slot = [0]

    def total_along(value, axis, size):
        base = loss_slot[0]
        loss_slot[0] += size
        loss_out_buf[base] = value
        copies = [
            send(loss_out_buf.at[base], loss_in_buf.at[base + d], **{axis: d}) for d in range(1, size)
        ]

        def finish():
            out = value
            for d, m in enumerate(copies, 1):
                m.wait_recv()
                out = out + loss_in_buf[base + d]
            return out

        return finish

    weigh(3)
    far_stage(0)
    far_stage(1)
    weigh(2)
    weigh(1)
    weigh(0)
    passage_term(7)
    near_term(0, 0)
    near_term(0, 1)
    z_far()
    near_send(0, 0, 1)
    near_send(0, 1, -1)
    passage_term(5)
    passage_term(6)
    near_term(1, 0)
    near_term(1, 1)
    near_send(1, 0, 1)
    near_send(1, 1, -1)
    z_near(3)
    finish = total_along(share * (1.0 / 16.0) - 2.0 * positive[...], "dx", 4)
    passage_term(3)
    passage_term(4)
    query_term(0)
    z_near(2)
    finish = total_along(finish(), "dy", 4)
    query_term(1)
    passage_term(1)
    passage_term(2)
    own_stage(0)
    own_stage(1)
    finish = total_along(finish(), "dz", 8)
    z_near(1)
    passage_term(0)
    finish = total_along(finish(), "dc", 2)
    near2_stage(0)
    near2_stage(1)
    total = finish()
    loss_out[...] = jnp.sum(jnp.sum(total, axis=1, keepdims=True), axis=0, keepdims=True) * (LN2 / (2.0 * PAIRS))
    query_out(0)
    query_out(1)
    passage_out()
    for copy in sent:
        copy.wait_send()


def on_device(queries, passages, pair):
    vmem = pl.BlockSpec(memory_space=pltpu.VMEM)
    query_grad, passage_grad, loss = pl.pallas_call(
        kernel,
        out_shape=(
            jax.ShapeDtypeStruct((OWN, D), bf16),
            jax.ShapeDtypeStruct((OWN, D), bf16),
            jax.ShapeDtypeStruct((1, 1), f32),
        ),
        in_specs=[vmem] * 3,
        out_specs=[vmem] * 3,
        scratch_shapes=[
            pltpu.VMEM((ROWS, D), bf16),
            pltpu.VMEM((ROWS, D), bf16),
            pltpu.VMEM((ROWS, ROWS), f32),
            pltpu.VMEM((ROWS, ROWS), bf16),
            pltpu.VMEM((ROWS, ROWS), bf16),
            pltpu.VMEM((ROWS, 128), f32),
            pltpu.VMEM((ROWS, 128), f32),
            pltpu.VMEM((8, ROWS), f32),
            pltpu.VMEM((8, ROWS), f32),
            pltpu.VMEM((16, 40, 128), f32),
            pltpu.VMEM((16, 16, 128), f32),
            pltpu.VMEM((32, 128), f32),
            pltpu.VMEM((ROWS, 128), f32),
            pltpu.VMEM((ROWS, 128), f32),
            pltpu.VMEM((128, 128), f32),
            pltpu.VMEM((16, 128), f32),
            pltpu.VMEM((1, ROWS), f32),
            pltpu.VMEM((1, ROWS), f32),
            pltpu.VMEM((ROWS, D), f32),
            pltpu.VMEM((ROWS // 2, D), f32),
            pltpu.VMEM((2, 2, tiles(OWN, D), 16, 128), i16),
            pltpu.VMEM((2, 2, tiles(OWN, D), 16, 128), i16),
            pltpu.VMEM((2, 2, tiles(BUNDLE, D), 16, 128), i16),
            pltpu.VMEM((2, 2, tiles(BUNDLE, D), 16, 128), i16),
            pltpu.VMEM((2, 2, tiles(HALF, D // 2), 16, 128), i16),
            pltpu.VMEM((2, 2, tiles(HALF, D // 2), 16, 128), i16),
            pltpu.VMEM((2, 2, tiles(HALF, D), 16, 128), i16),
            pltpu.VMEM((2, 2, tiles(HALF, D), 16, 128), i16),
            pltpu.VMEM((2, tiles(HALF, D), 16, 128), i16),
            pltpu.VMEM((2, tiles(HALF, D), 16, 128), i16),
            pltpu.VMEM((3, 2, tiles(OWN, D), 16, 128), i16),
            pltpu.VMEM((3, 2, tiles(OWN, D), 16, 128), i16),
            pltpu.VMEM((18, 8, 128), f32),
            pltpu.VMEM((18, 8, 128), f32),
            pltpu.VMEM((8, 128), f32),
            pltpu.SemaphoreType.DMA((MESSAGES,)),
            pltpu.SemaphoreType.DMA((MESSAGES,)),
        ],
        compiler_params=pltpu.CompilerParams(
            collective_id=0, has_side_effects=True, vmem_limit_bytes=60 * 1024 * 1024
        ),
    )(queries, passages, pair.reshape(1, OWN))
    return query_grad, passage_grad, loss.reshape(())


def solution(mesh):
    in_specs = (P(("loop", "grp"), None), P(("grp", "loop"), None), P(("loop", "grp")))
    out_specs = (P(("loop", "grp"), None), P(("grp", "loop"), None), P())
    return jax.shard_map(
        on_device, mesh=mesh, in_specs=in_specs, out_specs=out_specs, check_vma=False
    )
```

```python
import functools
import math

import jax
import jax.numpy as jnp
from jax import lax
from jax.experimental import pallas as pl
from jax.experimental.pallas import tpu as pltpu
from jax.sharding import PartitionSpec as P

MESH = pl.DeviceIdType.MESH
D = 1024
OWN = 96
HALF = 48
ROWS = 1536
BUNDLE = 192
CHUNK = 384
COLS = 512
PAIRS = 24576
TO_LOG2 = 50.0 * math.log2(math.e)
LN2 = math.log(2.0)
GRAD_SCALE = 25.0
LEVELS = 32000.0
SMALLEST = 1e-30
LOWEST = -1e38
RING4 = (0, 1, -1, 2)
RING8 = (0, 1, -1, 2, -2, 3, -3, 4)
AT4 = {0: 0, 1: 1, -1: 2, 2: 3}
AT8 = {0: 0, 1: 1, -1: 2, 2: 3, -2: 4, 3: 5, -3: 6, 4: 7}
MESSAGES = 140
f32 = jnp.float32
bf16 = jnp.bfloat16
i16 = jnp.int16


def tiles(rows, cols):
    return (rows // 16) * (cols // 128) + 1


def kernel(
    q_in, p_in, pair_in, qg_out, pg_out, loss_out,
    q_all, p_all, pair_own, scores, w,
    row_peak, row_sum, col_peak, col_sum,
    row_stats, col_stats, row_lse, row_rep, pair_rep, order, col_lse, col_rep, col_index,
    term, sib, far_out, far_in, near_out, near_in, last_out, last_in,
    z_far_out, z_far_in, z_out, z_in, loss_out_buf, loss_in_buf, positive,
    send_sem, recv_sem, own_sem,
):
    loop = lax.axis_index("loop")
    grp = lax.axis_index("grp")
    core = lax.rem(grp, 2)
    x = lax.rem(lax.div(grp, 2), 4)
    y = lax.div(loop, 8) * 2 + lax.div(grp, 8)
    z = lax.rem(loop, 8)

    def device(dx=0, dy=0, dz=0, dc=0):
        x2, y2 = lax.rem(x + dx + 4, 4), lax.rem(y + dy + 4, 4)
        z2, c2 = lax.rem(z + dz + 8, 8), lax.rem(core + dc, 2)
        return {
            "loop": lax.div(y2, 2) * 8 + z2,
            "grp": (lax.rem(y2, 2) * 4 + x2) * 2 + c2,
        }

    plane = [(dx, dy) for dx in range(4) for dy in range(4) if dx or dy]
    column = [(dz, dc) for dz in range(8) for dc in range(2) if dz or dc]

    barrier = pltpu.get_barrier_semaphore()
    neighbours = [{"dx": 1}, {"dx": -1}, {"dy": 1}, {"dy": -1}, {"dz": 1}, {"dz": -1}, {"dc": 1}]
    for where in neighbours:
        pl.semaphore_signal(barrier, inc=1, device_id=device(**where), device_id_type=MESH)
    own = [
        pltpu.make_async_copy(src, dst, own_sem.at[k])
        for k, (src, dst) in enumerate(
            (
                (q_in.at[pl.ds(0, HALF), :], q_all.at[pl.ds(0, HALF), :]),
                (q_in.at[pl.ds(HALF, HALF), :], q_all.at[pl.ds(BUNDLE, HALF), :]),
                (p_in, p_all.at[pl.ds(0, OWN), :]),
                (pair_in, pair_own),
            )
        )
    ]
    for copy in own:
        copy.start()

    count = [0]
    sent = []

    def send(src, dst, **where):
        k = count[0]
        count[0] += 1
        copy = pltpu.make_async_remote_copy(
            src_ref=src, dst_ref=dst, send_sem=send_sem.at[k], recv_sem=recv_sem.at[k],
            device_id=device(**where), device_id_type=MESH,
        )
        copy.start()
        sent.append(copy)
        return copy

    def q_at(half, p, q, cols=(0, D)):
        return q_all.at[pl.ds((2 * p + half) * BUNDLE + q * HALF, HALF), pl.ds(*cols)]

    def p_at(pos, rel, h=None):
        start = pos * BUNDLE + rel * OWN
        if h is None:
            return p_all.at[pl.ds(start, OWN), :]
        return p_all.at[pl.ds(start + h * HALF, HALF), :]

    pl.semaphore_wait(barrier, len(neighbours))
    for copy in own:
        copy.wait()

    first_axis, second_axis = ("dx", "dy"), ("dy", "dx")
    zs = {}
    for sign in (1, -1):
        for h in (0, 1):
            zs[sign, 1, h] = send(p_at(0, 0, h), p_at(AT8[-sign], 0, h), dz=sign)
    near1, far1, near2, far2 = {}, {}, {}, {}
    for sign in (1, -1):
        for half in (0, 1):
            near1[half, sign] = send(q_at(half, 0, 0), q_at(half, 0, AT4[-sign]), **{first_axis[half]: sign})
    sibling = {0: send(p_at(0, 0), p_at(0, 1), dc=1)}

    def spread(half, q):
        for sign in (1, -1):
            near2[half, sign, q] = send(
                q_at(half, 0, q), q_at(half, AT4[-sign], q), **{second_axis[half]: sign}
            )

    for half in (0, 1):
        spread(half, 0)
    for half in (0, 1):
        for sign in (1, -1):
            q = AT4[-sign]
            near1[half, sign].wait_recv()
            cols = (0, D // 2) if sign == 1 else (D // 2, D // 2)
            far1[half, sign] = send(q_at(half, 0, q, cols), q_at(half, 0, 3, cols), **{first_axis[half]: sign})
            spread(half, q)

    def hop(k):
        for h in (0, 1):
            for sign in (1, -1):
                if k == 4 and h != (0 if sign == 1 else 1):
                    continue
                zs[sign, k, h].wait_recv()
                if k < 3 or (k == 3 and h == (0 if sign == 1 else 1)):
                    pos, to = AT8[-sign * k], AT8[-sign * (k + 1) if k < 3 else 4]
                    zs[sign, k + 1, h] = send(p_at(pos, 0, h), p_at(to, 0, h), dz=sign)
        for pos in (AT8[k], AT8[-k]) if k < 4 else (7,):
            sibling[pos] = send(p_at(pos, 0), p_at(pos, 1), dc=1)

    row_peak[...] = jnp.full(row_peak.shape, LOWEST, f32)
    row_sum[...] = jnp.zeros(row_sum.shape, f32)
    col_peak[...] = jnp.full(col_peak.shape, LOWEST, f32)
    col_sum[...] = jnp.zeros(col_sum.shape, f32)
    slot = x * 4 + y
    col_slot = z * 2 + core
    row_stats[slot] = jnp.zeros((40, 128), f32)
    col_stats[col_slot] = jnp.zeros((16, 128), f32)
    row_stats[slot, pl.ds(32, 1), pl.ds(0, OWN)] = pair_own[...].astype(f32)
    hop(1)
    for half in (0, 1):
        for sign in (1, -1):
            far1[half, sign].wait_recv()
        spread(half, 3)

    def block(p, k):
        rows = pl.ds(pl.multiple_of(p * CHUNK, CHUNK), CHUNK)
        cols = pl.ds(pl.multiple_of(k * COLS, COLS), COLS)
        s = lax.dot_general(
            q_all[rows, :], p_all[cols, :], (((1,), (1,)), ((), ())), preferred_element_type=f32
        ) * TO_LOG2
        scores[rows, cols] = s
        parts = [s[:, 128 * i : 128 * (i + 1)] for i in range(COLS // 128)]
        old = row_peak[rows, :]
        peak = functools.reduce(jnp.maximum, parts, old)
        total = row_sum[rows, :] * jnp.exp2(old - peak)
        for part in parts:
            total += jnp.exp2(part - peak)
        row_peak[rows, :] = peak
        row_sum[rows, :] = total
        s3 = s.reshape(CHUNK // 8, 8, COLS)
        old = col_peak[:, cols]
        peak = jnp.maximum(old, jnp.max(s3, axis=0))
        col_sum[:, cols] = col_sum[:, cols] * jnp.exp2(old - peak) + jnp.sum(jnp.exp2(s3 - peak[None]), axis=0)
        col_peak[:, cols] = peak

    def blocks(start, stop, k):
        def body(p, _):
            block(p, k)
            return 0

        lax.fori_loop(start, stop, body, 0)

    for pos in (0, 1, 2):
        sibling[pos].wait_recv()
    block(0, 0)
    hop(2)
    for q in range(4):
        for half in (0, 1):
            for sign in (1, -1):
                near2[half, sign, q].wait_recv()
                if (q < 2) == (sign == 1):
                    far2[half, q] = send(
                        q_at(half, AT4[-sign], q), q_at(half, 3, q), **{second_axis[half]: sign}
                    )
    blocks(1, 3, 0)
    hop(3)
    for pos in (3, 4, 5, 6):
        sibling[pos].wait_recv()
    blocks(0, 3, 1)
    hop(4)
    for half in (0, 1):
        for q in range(4):
            far2[half, q].wait_recv()

    def last(k, _):
        block(3, k)
        return 0

    lax.fori_loop(0, 2, last, 0)
    sibling[7].wait_recv()
    blocks(0, 4, 2)

    def piece(half, p, q):
        dx, dy = (RING4[q], RING4[p]) if half == 0 else (RING4[p], RING4[q])
        return lax.rem(x + dx + 4, 4) * 4 + lax.rem(y + dy + 4, 4)

    for b in range(8):
        p, half = b // 2, b % 2
        rows = pl.ds(b * BUNDLE, BUNDLE)
        lanes = row_peak[rows, :]
        peak = jnp.max(lanes, axis=1, keepdims=True)
        total = jnp.sum(row_sum[rows, :] * jnp.exp2(lanes - peak), axis=1, keepdims=True)
        lse = jnp.broadcast_to(peak + jnp.log(total) * (1.0 / LN2), (BUNDLE, 128)).T
        for q in range(4):
            row_stats[slot, pl.ds(half * 16 + piece(half, p, q), 1), pl.ds(0, HALF)] = lse[
                0:1, q * HALF : (q + 1) * HALF
            ]
    row_msgs = [send(row_stats.at[slot], row_stats.at[slot], dx=dx, dy=dy) for dx, dy in plane]

    def owner(pos, rel):
        return lax.rem(z + RING8[pos] + 8, 8) * 2 + lax.rem(core + rel, 2)

    peak = jnp.max(col_peak[...], axis=0, keepdims=True)
    total = jnp.sum(col_sum[...] * jnp.exp2(col_peak[...] - peak), axis=0, keepdims=True)
    lse = peak + jnp.log(total) * (1.0 / LN2)
    for pos in range(8):
        for rel in (0, 1):
            start = pos * BUNDLE + rel * OWN
            col_stats[col_slot, pl.ds(owner(pos, rel), 1), pl.ds(0, OWN)] = lse[:, start : start + OWN]
    col_msgs = [send(col_stats.at[col_slot], col_stats.at[col_slot], dz=dz, dc=dc) for dz, dc in column]

    j = lax.broadcasted_iota(jnp.int32, (1, ROWS), 1)
    part = lax.shift_right_logical(j * 683, 16)
    within = j - part * OWN
    pos = lax.shift_right_logical(part, 1)
    away = lax.shift_right_logical(pos + 1, 1)
    away = jnp.where((pos & 1) == 1, away, -away)
    z2 = (z + away + 8) & 7
    c2 = (core + part) & 1
    first = (lax.div(grp, 2) * 2 + c2) * 16 + lax.div(loop, 8) * 8 + z2
    col_index[...] = (first * OWN + within).astype(f32)

    for m in row_msgs:
        m.wait_recv()
    stats = row_stats[:, 0:32, :]
    peak = jnp.max(stats, axis=0)
    lse = peak + jnp.log(jnp.sum(jnp.exp2(stats - peak[None]), axis=0)) * (1.0 / LN2)
    row_lse[...] = lse
    lane = lax.broadcasted_iota(jnp.int32, (32, 128), 1)
    share = jnp.sum(jnp.where(lane < HALF, lse, 0.0).reshape(4, 8, 128), axis=0)
    order[pl.ds(64, 64), :] = jnp.zeros((64, 128), f32)
    for b in range(8):
        p, half = b // 2, b % 2
        for q in range(4):
            at = piece(half, p, q)
            order[pl.ds(4 * b + q, 1), :] = row_lse[pl.ds(half * 16 + at, 1), :]
            order[pl.ds(32 + 4 * b + q, 1), :] = row_stats[at, pl.ds(32, 1), :]
    turned = order[...].T
    for b in range(8):
        half = b % 2
        for q in range(4):
            n = 4 * b + q
            rows = pl.ds(n * HALF, HALF)
            row_rep[rows, :] = jnp.broadcast_to(turned[0:HALF, n : n + 1], (HALF, 128))
            pair_rep[rows, :] = jnp.broadcast_to(
                turned[half * HALF : (half + 1) * HALF, 32 + n : 33 + n], (HALF, 128)
            )

    for m in col_msgs:
        m.wait_recv()
    stats = col_stats[...]
    peak = jnp.max(stats, axis=0)
    lse = peak + jnp.log(jnp.sum(jnp.exp2(stats - peak[None]), axis=0)) * (1.0 / LN2)
    col_lse[...] = lse
    lane = lax.broadcasted_iota(jnp.int32, (16, 128), 1)
    share = share + jnp.sum(jnp.where(lane < OWN, lse, 0.0).reshape(2, 8, 128), axis=0)
    col_rep[...] = jnp.concatenate(
        [col_lse[pl.ds(owner(pos, rel), 1), :][:, 0:OWN] for pos in range(8) for rel in (0, 1)], axis=1
    )

    positive[...] = jnp.zeros((8, 128), f32)

    def weigh(ps, ks):
        def body(n, _):
            p = ps[0] + lax.div(n, ks[1] - ks[0])
            k = ks[0] + lax.rem(n, ks[1] - ks[0])
            rows = pl.ds(pl.multiple_of(p * CHUNK, CHUNK), CHUNK)
            cols = pl.ds(pl.multiple_of(k * CHUNK, CHUNK), CHUNK)
            s = scores[rows, cols]
            hit = jnp.concatenate([pair_rep[rows, :]] * 3, axis=1) == col_index[:, cols]
            weight = (
                jnp.exp2(s - jnp.concatenate([row_rep[rows, :]] * 3, axis=1))
                + jnp.exp2(s - col_rep[:, cols])
                - jnp.where(hit, 2.0, 0.0)
            )
            found = jnp.sum(jnp.where(hit, s, 0.0).reshape(CHUNK // 8, 8, CHUNK), axis=0)
            positive[...] += found[:, 0:128] + found[:, 128:256] + found[:, 256:384]
            w[rows, cols] = weight.astype(bf16)
            return 0

        lax.fori_loop(0, (ps[1] - ps[0]) * (ks[1] - ks[0]), body, 0)

    def query_term(p):
        rows = pl.ds(p * CHUNK, CHUNK)
        scores[rows, pl.ds(0, D)] = jnp.dot(w[rows, :], p_all[...], preferred_element_type=f32)

    sib_msgs = {}

    def passage_term(k):
        rows = pl.ds(k * CHUNK, CHUNK)
        term[rows, :] = lax.dot_general(
            w[:, rows], q_all[...], (((0,), (0,)), ((), ())), preferred_element_type=f32
        )
        for pos in (2 * k + 1, 2 * k):
            sib_msgs[pos] = send(
                term.at[pl.ds(pos * BUNDLE + OWN, OWN), :], sib.at[pl.ds(pos * OWN, OWN), :], dc=1
            )

    def add_sibling(pos):
        sib_msgs[pos].wait_recv()
        term[pl.ds(pos * BUNDLE, OWN), :] += sib[pl.ds(pos * OWN, OWN), :]

    def encode(ref, r0, rows, c0, cols, buf):
        peak = functools.reduce(
            jnp.maximum,
            [
                jnp.max(jnp.abs(ref[pl.ds(r0, rows), pl.ds(c0 + 128 * i, 128)]).reshape(rows // 8, 8, 128), axis=0)
                for i in range(cols // 128)
            ],
        )
        power = jnp.floor(jnp.log(jnp.maximum(peak, SMALLEST)) * (1.0 / LN2)) + 1.0
        factor = (jnp.exp2(-power) * LEVELS)[None]
        n = rows // 16
        for i in range(cols // 128):
            v = ref[pl.ds(r0, rows), pl.ds(c0 + 128 * i, 128)].reshape(rows // 8, 8, 128) * factor
            buf[pl.ds(i * n, n)] = jnp.round(v).astype(jnp.int32).reshape(n, 16, 128).astype(i16)
        both = jnp.concatenate([power, power], axis=0).astype(jnp.int32)
        buf[pl.ds(n * (cols // 128), 1)] = both.astype(i16)[None]

    def add_decoded(ref, r0, rows, c0, cols, buf):
        n = rows // 16
        power = buf[n * (cols // 128)].astype(jnp.int32).astype(f32)[0:8]
        factor = (jnp.exp2(power) * (1.0 / LEVELS))[None]
        for i in range(cols // 128):
            v = buf[pl.ds(i * n, n)].astype(jnp.int32).astype(f32).reshape(rows // 8, 8, 128) * factor
            ref[pl.ds(r0, rows), pl.ds(c0 + 128 * i, 128)] += v.reshape(rows, 128)

    msgs = {}

    def far_send():
        for half in (0, 1):
            for sign, s in ((1, 0), (-1, 1)):
                encode(scores, 3 * CHUNK + half * BUNDLE + s * OWN, OWN, 0, D, far_out.at[half, s])
                msgs["far", half, s] = send(
                    far_out.at[half, s], far_in.at[half, s], **{second_axis[half]: sign}
                )

    def near_send(part):
        for half in (0, 1):
            for sign, s in ((1, 0), (-1, 1)):
                side = s if part else 1 - s
                row = (1 + s) * CHUNK + half * BUNDLE + side * OWN
                if part:
                    msgs["far", half, s].wait_recv()
                    add_decoded(scores, row, OWN, 0, D, far_in.at[half, s])
                encode(scores, row, OWN, 0, D, near_out.at[half, s, part])
                msgs["near", half, s, part] = send(
                    near_out.at[half, s, part], near_in.at[half, s, part], **{second_axis[half]: sign}
                )

    def own_add(part):
        for half in (0, 1):
            for s in (0, 1):
                side = s if part else 1 - s
                msgs["near", half, s, part].wait_recv()
                add_decoded(scores, half * BUNDLE + side * OWN, OWN, 0, D, near_in.at[half, s, part])

    def last_send():
        for half in (0, 1):
            for q in (3, 2, 1):
                encode(scores, half * BUNDLE + q * HALF, HALF, 0, D, last_out.at[half, q - 1])
                msgs["last", half, q] = send(
                    last_out.at[half, q - 1], last_in.at[half, q - 1], **{first_axis[half]: RING4[q]}
                )

    def query_out():
        for half in (0, 1):
            row = half * BUNDLE
            for q in (1, 2, 3):
                msgs["last", half, q].wait_recv()
                add_decoded(scores, row, HALF, 0, D, last_in.at[half, q - 1])
            qg_out[pl.ds(half * HALF, HALF), :] = (scores[pl.ds(row, HALF), pl.ds(0, D)] * GRAD_SCALE).astype(bf16)

    def z_far():
        add_sibling(7)
        for sign, s in ((1, 0), (-1, 1)):
            encode(term, 7 * BUNDLE + s * HALF, HALF, 0, D, z_far_out.at[s])
            msgs["z", 4, s] = send(z_far_out.at[s], z_far_in.at[s], dz=sign)

    def z_near(k):
        for s in (0, 1):
            add_sibling(AT8[(1 - 2 * s) * k])
        for part in (0, 1):
            for sign, s in ((1, 0), (-1, 1)):
                row = AT8[sign * k] * BUNDLE + (s if part else 1 - s) * HALF
                if k < 3:
                    msgs["z", k + 1, s, part].wait_recv()
                    add_decoded(term, row, HALF, 0, D, z_in.at[k, s, part])
                elif part:
                    msgs["z", 4, s].wait_recv()
                    add_decoded(term, row, HALF, 0, D, z_far_in.at[s])
                encode(term, row, HALF, 0, D, z_out.at[k - 1, s, part])
                msgs["z", k, s, part] = send(z_out.at[k - 1, s, part], z_in.at[k - 1, s, part], dz=sign)

    def passage_out():
        add_sibling(0)
        for part in (0, 1):
            for s in (0, 1):
                msgs["z", 1, s, part].wait_recv()
                add_decoded(term, (s if part else 1 - s) * HALF, HALF, 0, D, z_in.at[0, s, part])
        pg_out[...] = (term[pl.ds(0, OWN), :] * GRAD_SCALE).astype(bf16)

    loss_slot = [0]

    def total_along(value, axis, size):
        base = loss_slot[0]
        loss_slot[0] += size
        loss_out_buf[base] = value
        copies = [
            send(loss_out_buf.at[base], loss_in_buf.at[base + d], **{axis: d}) for d in range(1, size)
        ]

        def finish():
            out = value
            for d, m in enumerate(copies, 1):
                m.wait_recv()
                out = out + loss_in_buf[base + d]
            return out

        return finish

    weigh((0, 4), (3, 4))
    passage_term(3)
    weigh((3, 4), (0, 3))
    query_term(3)
    far_send()
    z_far()
    weigh((0, 3), (2, 3))
    passage_term(2)
    weigh((1, 3), (0, 2))
    query_term(1)
    query_term(2)
    near_send(0)
    z_near(3)
    near_send(1)
    weigh((0, 1), (0, 2))
    finish = total_along(share * (1.0 / 16.0) - 2.0 * positive[...], "dx", 4)
    passage_term(1)
    query_term(0)
    z_near(2)
    finish = total_along(finish(), "dy", 4)
    own_add(0)
    passage_term(0)
    own_add(1)
    last_send()
    finish = total_along(finish(), "dz", 8)
    z_near(1)
    finish = total_along(finish(), "dc", 2)
    query_out()
    total = finish()
    loss_out[...] = jnp.sum(jnp.sum(total, axis=1, keepdims=True), axis=0, keepdims=True) * (LN2 / (2.0 * PAIRS))
    passage_out()
    for copy in sent:
        copy.wait_send()


def on_device(queries, passages, pair):
    vmem = pl.BlockSpec(memory_space=pltpu.VMEM)
    anywhere = pl.BlockSpec(memory_space=pl.ANY)
    query_grad, passage_grad, loss = pl.pallas_call(
        kernel,
        out_shape=(
            pltpu.VMEM((OWN, D), bf16),
            pltpu.VMEM((OWN, D), bf16),
            jax.ShapeDtypeStruct((1, 1), f32),
        ),
        in_specs=[anywhere] * 3,
        out_specs=[vmem] * 3,
        scratch_shapes=[
            pltpu.VMEM((ROWS, D), bf16),
            pltpu.VMEM((ROWS, D), bf16),
            pltpu.VMEM((1, OWN), jnp.int32),
            pltpu.VMEM((ROWS, ROWS), f32),
            pltpu.VMEM((ROWS, ROWS), bf16),
            pltpu.VMEM((ROWS, 128), f32),
            pltpu.VMEM((ROWS, 128), f32),
            pltpu.VMEM((8, ROWS), f32),
            pltpu.VMEM((8, ROWS), f32),
            pltpu.VMEM((16, 40, 128), f32),
            pltpu.VMEM((16, 16, 128), f32),
            pltpu.VMEM((32, 128), f32),
            pltpu.VMEM((ROWS, 128), f32),
            pltpu.VMEM((ROWS, 128), f32),
            pltpu.VMEM((128, 128), f32),
            pltpu.VMEM((16, 128), f32),
            pltpu.VMEM((1, ROWS), f32),
            pltpu.VMEM((1, ROWS), f32),
            pltpu.VMEM((ROWS, D), f32),
            pltpu.VMEM((ROWS // 2, D), f32),
            pltpu.VMEM((2, 2, tiles(OWN, D), 16, 128), i16),
            pltpu.VMEM((2, 2, tiles(OWN, D), 16, 128), i16),
            pltpu.VMEM((2, 2, 2, tiles(OWN, D), 16, 128), i16),
            pltpu.VMEM((2, 2, 2, tiles(OWN, D), 16, 128), i16),
            pltpu.VMEM((2, 3, tiles(HALF, D), 16, 128), i16),
            pltpu.VMEM((2, 3, tiles(HALF, D), 16, 128), i16),
            pltpu.VMEM((2, tiles(HALF, D), 16, 128), i16),
            pltpu.VMEM((2, tiles(HALF, D), 16, 128), i16),
            pltpu.VMEM((3, 2, 2, tiles(HALF, D), 16, 128), i16),
            pltpu.VMEM((3, 2, 2, tiles(HALF, D), 16, 128), i16),
            pltpu.VMEM((18, 8, 128), f32),
            pltpu.VMEM((18, 8, 128), f32),
            pltpu.VMEM((8, 128), f32),
            pltpu.SemaphoreType.DMA((MESSAGES,)),
            pltpu.SemaphoreType.DMA((MESSAGES,)),
            pltpu.SemaphoreType.DMA((4,)),
        ],
        compiler_params=pltpu.CompilerParams(
            collective_id=0, has_side_effects=True, vmem_limit_bytes=60 * 1024 * 1024
        ),
    )(queries, passages, pair.reshape(1, OWN))
    return query_grad, passage_grad, loss.reshape(())


def solution(mesh):
    in_specs = (P(("loop", "grp"), None), P(("grp", "loop"), None), P(("loop", "grp")))
    out_specs = (P(("loop", "grp"), None), P(("grp", "loop"), None), P())
    return jax.shard_map(
        on_device, mesh=mesh, in_specs=in_specs, out_specs=out_specs, check_vma=False
    )
```

```python
import functools
import math

import jax
import jax.numpy as jnp
from jax import lax
from jax.experimental import pallas as pl
from jax.experimental.pallas import tpu as pltpu
from jax.sharding import PartitionSpec as P

MESH = pl.DeviceIdType.MESH
D = 1024
OWN = 96
HALF = 48
ROWS = 1536
BUNDLE = 192
CHUNK = 384
COLS = 512
PAIRS = 24576
TO_LOG2 = 50.0 * math.log2(math.e)
LN2 = math.log(2.0)
GRAD_SCALE = 25.0
LEVELS = 32000.0
SMALLEST = 1e-30
LOWEST = -1e38
RING4 = (0, 1, -1, 2)
RING8 = (0, 1, -1, 2, -2, 3, -3, 4)
AT4 = {0: 0, 1: 1, -1: 2, 2: 3}
AT8 = {0: 0, 1: 1, -1: 2, 2: 3, -2: 4, 3: 5, -3: 6, 4: 7}
MESSAGES = 144
f32 = jnp.float32
bf16 = jnp.bfloat16
i16 = jnp.int16


def tiles(rows, cols):
    return (rows // 16) * (cols // 128) + 1


def kernel(
    q_in, p_in, pair_in, qg_out, pg_out, loss_out,
    q_all, p_all, pair_own, scores, w,
    row_peak, row_sum, col_peak, col_sum,
    row_stats, col_stats, row_lse, row_rep, pair_rep, order, col_lse, col_rep, col_index,
    term, sib, far_out, far_in, near_out, near_in, rest_out, rest_in, last_out, last_in,
    z_far_out, z_far_in, z_out, z_in, loss_out_buf, loss_in_buf, positive,
    send_sem, recv_sem, own_sem,
):
    loop = lax.axis_index("loop")
    grp = lax.axis_index("grp")
    core = lax.rem(grp, 2)
    x = lax.rem(lax.div(grp, 2), 4)
    y = lax.div(loop, 8) * 2 + lax.div(grp, 8)
    z = lax.rem(loop, 8)

    xs = [x] + [lax.rem(x + d, 4) for d in (1, 2, 3)]
    ys = [y] + [lax.rem(y + d, 4) for d in (1, 2, 3)]
    zs8 = [z] + [lax.rem(z + d, 8) for d in range(1, 8)]
    cores = [core, 1 - core]
    y_loop = [lax.div(v, 2) * 8 for v in ys]
    y_grp = [lax.rem(v, 2) * 8 for v in ys]

    def device(dx=0, dy=0, dz=0, dc=0):
        return {
            "loop": y_loop[dy % 4] + zs8[dz % 8],
            "grp": y_grp[dy % 4] + xs[dx % 4] * 2 + cores[dc],
        }

    def hops(d, size):
        return min(d, size - d)

    plane = [(dx, dy) for dx in range(4) for dy in range(4) if dx or dy]
    plane.sort(key=lambda d: -hops(d[0], 4) - hops(d[1], 4))
    column = [(dz, dc) for dz in range(8) for dc in range(2) if dz or dc]
    column.sort(key=lambda d: -hops(d[0], 8) * 2 - d[1])

    barrier = pltpu.get_barrier_semaphore()
    neighbours = [{"dx": 1}, {"dx": -1}, {"dy": 1}, {"dy": -1}, {"dz": 1}, {"dz": -1}, {"dc": 1}]
    for where in neighbours:
        pl.semaphore_signal(barrier, inc=1, device_id=device(**where), device_id_type=MESH)
    own = [
        pltpu.make_async_copy(src, dst, own_sem.at[k])
        for k, (src, dst) in enumerate(
            (
                (q_in.at[pl.ds(0, HALF), :], q_all.at[pl.ds(0, HALF), :]),
                (q_in.at[pl.ds(HALF, HALF), :], q_all.at[pl.ds(BUNDLE, HALF), :]),
                (p_in, p_all.at[pl.ds(0, OWN), :]),
                (pair_in, pair_own),
            )
        )
    ]
    for copy in own:
        copy.start()

    count = [0]
    sent = []

    def send(src, dst, **where):
        k = count[0]
        count[0] += 1
        copy = pltpu.make_async_remote_copy(
            src_ref=src, dst_ref=dst, send_sem=send_sem.at[k], recv_sem=recv_sem.at[k],
            device_id=device(**where), device_id_type=MESH,
        )
        copy.start()
        sent.append(copy)
        return copy

    def q_at(half, p, q, cols=(0, D)):
        return q_all.at[pl.ds((2 * p + half) * BUNDLE + q * HALF, HALF), pl.ds(*cols)]

    def p_at(pos, rel, h=None):
        start = pos * BUNDLE + rel * OWN
        if h is None:
            return p_all.at[pl.ds(start, OWN), :]
        return p_all.at[pl.ds(start + h * HALF, HALF), :]

    pl.semaphore_wait(barrier, len(neighbours))
    for copy in own:
        copy.wait()

    first_axis, second_axis = ("dx", "dy"), ("dy", "dx")
    zs, near1, far1, near2, far2, sibling = {}, {}, {}, {}, {}, {}

    def spread(half, q):
        for sign in (1, -1):
            near2[half, sign, q] = send(
                q_at(half, 0, q), q_at(half, AT4[-sign], q), **{second_axis[half]: sign}
            )

    def z_own(h):
        for sign in (1, -1):
            zs[sign, 1, h] = send(p_at(0, 0, h), p_at(AT8[-sign], 0, h), dz=sign)

    def z_pass(k, h):
        for sign in (1, -1):
            last = h != (0 if sign == 1 else 1)
            if k == 4 and last:
                continue
            zs[sign, k, h].wait_recv()
            if k < 3 or (k == 3 and not last):
                pos, to = AT8[-sign * k], AT8[-sign * (k + 1)] if k < 3 else 7
                zs[sign, k + 1, h] = send(p_at(pos, 0, h), p_at(to, 0, h), dz=sign)

    def to_sibling(*positions):
        for pos in positions:
            sibling[pos] = send(p_at(pos, 0), p_at(pos, 1), dc=1)

    def pass_far(q):
        for half in (0, 1):
            for sign in (1, -1):
                near2[half, sign, q].wait_recv()
                if (q < 2) == (sign == 1):
                    far2[half, q] = send(
                        q_at(half, AT4[-sign], q), q_at(half, 3, q), **{second_axis[half]: sign}
                    )

    for half in (0, 1):
        for sign in (1, -1):
            near1[half, sign] = send(q_at(half, 0, 0), q_at(half, 0, AT4[-sign]), **{first_axis[half]: sign})
    z_own(0)
    for half in (0, 1):
        spread(half, 0)
    z_own(1)
    to_sibling(0)
    row_peak[...] = jnp.full(row_peak.shape, LOWEST, f32)
    row_sum[...] = jnp.zeros(row_sum.shape, f32)
    col_peak[...] = jnp.full(col_peak.shape, LOWEST, f32)
    col_sum[...] = jnp.zeros(col_sum.shape, f32)
    slot = x * 4 + y
    col_slot = z * 2 + core
    row_stats[slot] = jnp.zeros((40, 128), f32)
    col_stats[col_slot] = jnp.zeros((16, 128), f32)
    row_stats[slot, pl.ds(32, 1), pl.ds(0, OWN)] = pair_own[...].astype(f32)

    z_pass(1, 0)
    for half in (0, 1):
        for sign in (1, -1):
            q = AT4[-sign]
            near1[half, sign].wait_recv()
            cols = (0, D // 2) if sign == 1 else (D // 2, D // 2)
            far1[half, sign] = send(q_at(half, 0, q, cols), q_at(half, 0, 3, cols), **{first_axis[half]: sign})
            spread(half, q)
    z_pass(1, 1)
    to_sibling(1, 2)
    pass_far(0)
    for half in (0, 1):
        for sign in (1, -1):
            far1[half, sign].wait_recv()
        spread(half, 3)
    z_pass(2, 0)

    def block(p, start, width):
        rows = pl.ds(p * CHUNK, CHUNK)
        cols = pl.ds(start, width)
        s = lax.dot_general(
            q_all[rows, :], p_all[cols, :], (((1,), (1,)), ((), ())), preferred_element_type=f32
        ) * TO_LOG2
        scores[rows, cols] = s
        parts = [s[:, 128 * i : 128 * (i + 1)] for i in range(width // 128)]
        old = row_peak[rows, :]
        peak = functools.reduce(jnp.maximum, parts, old)
        total = row_sum[rows, :] * jnp.exp2(old - peak)
        for part in parts:
            total += jnp.exp2(part - peak)
        row_peak[rows, :] = peak
        row_sum[rows, :] = total
        s3 = s.reshape(CHUNK // 8, 8, width)
        old = col_peak[:, cols]
        peak = jnp.maximum(old, jnp.max(s3, axis=0))
        col_sum[:, cols] = col_sum[:, cols] * jnp.exp2(old - peak) + jnp.sum(jnp.exp2(s3 - peak[None]), axis=0)
        col_peak[:, cols] = peak

    for pos in (0, 1, 2):
        sibling[pos].wait_recv()
    block(0, 0, 512)
    pass_far(1)
    z_pass(2, 1)
    to_sibling(3, 4)
    pass_far(2)
    z_pass(3, 0)
    pass_far(3)
    block(1, 0, 512)
    z_pass(3, 1)
    to_sibling(5, 6)
    block(2, 0, 512)
    for pos in (3, 4, 5, 6):
        sibling[pos].wait_recv()
    block(0, 512, 512)
    z_pass(4, 0)
    z_pass(4, 1)
    to_sibling(7)
    block(1, 512, 512)
    block(2, 512, 512)
    for half in (0, 1):
        for q in range(4):
            far2[half, q].wait_recv()
    block(3, 0, 1024)
    sibling[7].wait_recv()

    def piece(half, p, q):
        dx, dy = (RING4[q], RING4[p]) if half == 0 else (RING4[p], RING4[q])
        return xs[dx % 4] * 4 + ys[dy % 4]

    def owner(pos, rel):
        return zs8[RING8[pos] % 8] * 2 + cores[rel]

    def finish_rows(p):
        rows = pl.ds(p * CHUNK, CHUNK)
        lanes = row_peak[rows, :].T
        peak = jnp.max(lanes, axis=0, keepdims=True)
        total = jnp.sum(row_sum[rows, :].T * jnp.exp2(lanes - peak), axis=0, keepdims=True)
        lse = peak + jnp.log(total) * (1.0 / LN2)
        for half in (0, 1):
            for q in range(4):
                start = half * BUNDLE + q * HALF
                row_stats[slot, pl.ds(half * 16 + piece(half, p, q), 1), pl.ds(0, HALF)] = lse[:, start : start + HALF]

    block(0, 1024, 512)
    block(1, 1024, 512)
    finish_rows(0)
    block(2, 1024, 512)
    finish_rows(1)
    block(3, 1024, 512)
    finish_rows(2)
    peak = jnp.max(col_peak[...], axis=0, keepdims=True)
    total = jnp.sum(col_sum[...] * jnp.exp2(col_peak[...] - peak), axis=0, keepdims=True)
    lse = peak + jnp.log(total) * (1.0 / LN2)
    for pos in range(8):
        for rel in (0, 1):
            start = pos * BUNDLE + rel * OWN
            col_stats[col_slot, pl.ds(owner(pos, rel), 1), pl.ds(0, OWN)] = lse[:, start : start + OWN]
    finish_rows(3)
    row_msgs, col_msgs = [], []
    for (dx, dy), (dz, dc) in zip(plane, column, strict=True):
        row_msgs.append(send(row_stats.at[slot], row_stats.at[slot], dx=dx, dy=dy))
        col_msgs.append(send(col_stats.at[col_slot], col_stats.at[col_slot], dz=dz, dc=dc))

    j = lax.broadcasted_iota(jnp.int32, (1, ROWS), 1)
    part = lax.shift_right_logical(j * 683, 16)
    within = j - part * OWN
    pos = lax.shift_right_logical(part, 1)
    away = lax.shift_right_logical(pos + 1, 1)
    away = jnp.where((pos & 1) == 1, away, -away)
    z2 = (z + away + 8) & 7
    c2 = (core + part) & 1
    first = (lax.div(grp, 2) * 2 + c2) * 16 + lax.div(loop, 8) * 8 + z2
    col_index[...] = (first * OWN + within).astype(f32)

    for m in row_msgs:
        m.wait_recv()
    stats = row_stats[:, 0:32, :]
    peak = jnp.max(stats, axis=0)
    lse = peak + jnp.log(jnp.sum(jnp.exp2(stats - peak[None]), axis=0)) * (1.0 / LN2)
    row_lse[...] = lse
    lane = lax.broadcasted_iota(jnp.int32, (32, 128), 1)
    share = jnp.sum(jnp.where(lane < HALF, lse, 0.0).reshape(4, 8, 128), axis=0)
    order[pl.ds(64, 64), :] = jnp.zeros((64, 128), f32)
    for b in range(8):
        p, half = b // 2, b % 2
        for q in range(4):
            at = piece(half, p, q)
            order[pl.ds(4 * b + q, 1), :] = row_lse[pl.ds(half * 16 + at, 1), :]
            order[pl.ds(32 + 4 * b + q, 1), :] = row_stats[at, pl.ds(32, 1), :]
    turned = order[...].T
    for b in range(8):
        half = b % 2
        for q in range(4):
            n = 4 * b + q
            rows = pl.ds(n * HALF, HALF)
            row_rep[rows, :] = jnp.broadcast_to(turned[0:HALF, n : n + 1], (HALF, 128))
            pair_rep[rows, :] = jnp.broadcast_to(
                turned[half * HALF : (half + 1) * HALF, 32 + n : 33 + n], (HALF, 128)
            )

    for m in col_msgs:
        m.wait_recv()
    stats = col_stats[...]
    peak = jnp.max(stats, axis=0)
    lse = peak + jnp.log(jnp.sum(jnp.exp2(stats - peak[None]), axis=0)) * (1.0 / LN2)
    col_lse[...] = lse
    lane = lax.broadcasted_iota(jnp.int32, (16, 128), 1)
    share = share + jnp.sum(jnp.where(lane < OWN, lse, 0.0).reshape(2, 8, 128), axis=0)
    col_rep[...] = jnp.concatenate(
        [col_lse[pl.ds(owner(pos, rel), 1), :][:, 0:OWN] for pos in range(8) for rel in (0, 1)], axis=1
    )

    positive[...] = jnp.zeros((8, 128), f32)

    def weigh(p, k):
        rows, cols = pl.ds(p * CHUNK, CHUNK), pl.ds(k * CHUNK, CHUNK)
        s = scores[rows, cols]
        hit = jnp.concatenate([pair_rep[rows, :]] * 3, axis=1) == col_index[:, cols]
        weight = (
            jnp.exp2(s - jnp.concatenate([row_rep[rows, :]] * 3, axis=1))
            + jnp.exp2(s - col_rep[:, cols])
            - jnp.where(hit, 2.0, 0.0)
        )
        found = jnp.sum(jnp.where(hit, s, 0.0).reshape(CHUNK // 8, 8, CHUNK), axis=0)
        positive[...] += found[:, 0:128] + found[:, 128:256] + found[:, 256:384]
        w[rows, cols] = weight.astype(bf16)

    def query_term(p):
        rows = pl.ds(p * CHUNK, CHUNK)
        scores[rows, pl.ds(0, D)] = jnp.dot(w[rows, :], p_all[...], preferred_element_type=f32)

    def near_rows(half, s, side):
        return (1 + s) * CHUNK + half * BUNDLE + side * OWN

    def near_terms(part):
        starts = [near_rows(half, s, s if part else 1 - s) for half in (0, 1) for s in (0, 1)]
        rows = jnp.concatenate([w[pl.ds(start, OWN), :] for start in starts], axis=0)
        out = jnp.dot(rows, p_all[...], preferred_element_type=f32)
        for i, start in enumerate(starts):
            scores[pl.ds(start, OWN), pl.ds(0, D)] = out[i * OWN : (i + 1) * OWN, :]

    sib_msgs = {}

    def passage_term(k):
        rows = pl.ds(k * CHUNK, CHUNK)
        term[rows, :] = lax.dot_general(
            w[:, rows], q_all[...], (((0,), (0,)), ((), ())), preferred_element_type=f32
        )

    def sib_send(k):
        for pos in (2 * k + 1, 2 * k):
            sib_msgs[pos] = send(
                term.at[pl.ds(pos * BUNDLE + OWN, OWN), :], sib.at[pl.ds(pos * OWN, OWN), :], dc=1
            )

    def add_sibling(*positions):
        for pos in positions:
            sib_msgs[pos].wait_recv()
        for pos in positions:
            term[pl.ds(pos * BUNDLE, OWN), :] += sib[pl.ds(pos * OWN, OWN), :]

    def encode(ref, r0, rows, c0, cols, buf):
        peak = functools.reduce(
            jnp.maximum,
            [
                jnp.max(jnp.abs(ref[pl.ds(r0, rows), pl.ds(c0 + 128 * i, 128)]).reshape(rows // 8, 8, 128), axis=0)
                for i in range(cols // 128)
            ],
        )
        power = jnp.floor(jnp.log(jnp.maximum(peak, SMALLEST)) * (1.0 / LN2)) + 1.0
        factor = (jnp.exp2(-power) * LEVELS)[None]
        n = rows // 16
        for i in range(cols // 128):
            v = ref[pl.ds(r0, rows), pl.ds(c0 + 128 * i, 128)].reshape(rows // 8, 8, 128) * factor
            buf[pl.ds(i * n, n)] = jnp.round(v).astype(jnp.int32).reshape(n, 16, 128).astype(i16)
        both = jnp.concatenate([power, power], axis=0).astype(jnp.int32)
        buf[pl.ds(n * (cols // 128), 1)] = both.astype(i16)[None]

    def add_decoded(ref, r0, rows, c0, cols, buf):
        n = rows // 16
        power = buf[n * (cols // 128)].astype(jnp.int32).astype(f32)[0:8]
        factor = (jnp.exp2(power) * (1.0 / LEVELS))[None]
        for i in range(cols // 128):
            v = buf[pl.ds(i * n, n)].astype(jnp.int32).astype(f32).reshape(rows // 8, 8, 128) * factor
            ref[pl.ds(r0, rows), pl.ds(c0 + 128 * i, 128)] += v.reshape(rows, 128)

    msgs = {}
    sides = [(half, sign, s) for half in (0, 1) for sign, s in ((1, 0), (-1, 1))]

    def far_send():
        for half, _, s in sides:
            encode(scores, 3 * CHUNK + half * BUNDLE + s * OWN, OWN, 0, D, far_out.at[half, s])
        for half, sign, s in sides:
            msgs["far", half, s] = send(far_out.at[half, s], far_in.at[half, s], **{second_axis[half]: sign})

    def near_send():
        for half, _, s in sides:
            encode(scores, near_rows(half, s, 1 - s), OWN, 0, D, near_out.at[half, s])
        for half, sign, s in sides:
            msgs["near", half, s] = send(near_out.at[half, s], near_in.at[half, s], **{second_axis[half]: sign})

    def far_wait():
        for half, _, s in sides:
            msgs["far", half, s].wait_recv()

    def rest_encode():
        for half, _, s in sides:
            row = near_rows(half, s, s)
            add_decoded(scores, row, OWN, 0, D, far_in.at[half, s])
            for u in (0, 1):
                encode(scores, row + (1 - u) * HALF, HALF, 0, D, rest_out.at[half, s, u])

    def rest_send():
        for u in (0, 1):
            for half, sign, s in sides:
                msgs["rest", half, s, u] = send(
                    rest_out.at[half, s, u], rest_in.at[half, s, u], **{second_axis[half]: sign}
                )

    def near_add():
        for half, _, s in sides:
            msgs["near", half, s].wait_recv()
        for half, _, s in sides:
            add_decoded(scores, half * BUNDLE + (1 - s) * OWN, OWN, 0, D, near_in.at[half, s])

    def rest_add(u):
        for half, _, s in sides:
            msgs["rest", half, s, u].wait_recv()
        for half, _, s in sides:
            add_decoded(scores, half * BUNDLE + s * OWN + (1 - u) * HALF, HALF, 0, D, rest_in.at[half, s, u])

    def last_send(*qs):
        for half in (0, 1):
            for q in qs:
                encode(scores, half * BUNDLE + q * HALF, HALF, 0, D, last_out.at[half, q - 1])
        for q in qs:
            for half in (0, 1):
                msgs["last", half, q] = send(
                    last_out.at[half, q - 1], last_in.at[half, q - 1], **{first_axis[half]: RING4[q]}
                )

    def query_out():
        for q in (1, 3, 2):
            for half in (0, 1):
                msgs["last", half, q].wait_recv()
            for half in (0, 1):
                add_decoded(scores, half * BUNDLE, HALF, 0, D, last_in.at[half, q - 1])
        for half in (0, 1):
            rows = pl.ds(half * BUNDLE, HALF)
            qg_out[pl.ds(half * HALF, HALF), :] = (scores[rows, pl.ds(0, D)] * GRAD_SCALE).astype(bf16)

    def z_far():
        for s in (0, 1):
            encode(term, 7 * BUNDLE + s * HALF, HALF, 0, D, z_far_out.at[s])
        for sign, s in ((1, 0), (-1, 1)):
            msgs["z", 4, s] = send(z_far_out.at[s], z_far_in.at[s], dz=sign)

    def z_near(k, part):
        rows = [AT8[sign * k] * BUNDLE + (s if part else 1 - s) * HALF for sign, s in ((1, 0), (-1, 1))]
        if k < 3:
            arrived = [(msgs["z", k + 1, s, part], z_in.at[k, s, part]) for s in (0, 1)]
        else:
            arrived = [(msgs["z", 4, s], z_far_in.at[s]) for s in (0, 1)] if part else []
        for message, _ in arrived:
            message.wait_recv()
        for row, (_, buf) in zip(rows, arrived):
            add_decoded(term, row, HALF, 0, D, buf)
        for s in (0, 1):
            encode(term, rows[s], HALF, 0, D, z_out.at[k - 1, s, part])
        for sign, s in ((1, 0), (-1, 1)):
            msgs["z", k, s, part] = send(z_out.at[k - 1, s, part], z_in.at[k - 1, s, part], dz=sign)

    def passage_out():
        for part in (0, 1):
            for s in (0, 1):
                msgs["z", 1, s, part].wait_recv()
            for s in (0, 1):
                add_decoded(term, (s if part else 1 - s) * HALF, HALF, 0, D, z_in.at[0, s, part])
        pg_out[...] = (term[pl.ds(0, OWN), :] * GRAD_SCALE).astype(bf16)

    loss_slot = [0]

    def total_along(value, axis, size):
        base = loss_slot[0]
        loss_slot[0] += size
        loss_out_buf[base] = value
        copies = [
            send(loss_out_buf.at[base], loss_in_buf.at[base + d], **{axis: d}) for d in range(1, size)
        ]

        def finish():
            out = value
            for d, m in enumerate(copies, 1):
                m.wait_recv()
                out = out + loss_in_buf[base + d]
            return out

        return finish

    for p in range(4):
        weigh(p, 3)
    passage_term(3)
    for k in range(3):
        weigh(3, k)
    sib_send(3)
    query_term(3)
    for p in (1, 2):
        for k in range(3):
            weigh(p, k)
    far_send()
    add_sibling(7)
    z_far()
    near_terms(0)
    for k in (2, 1, 0):
        weigh(0, k)
    near_send()
    passage_term(2)
    sib_send(2)
    near_terms(1)
    add_sibling(5, 6)
    z_near(3, 0)
    z_near(3, 1)
    finish = total_along(share * (1.0 / 16.0) - 2.0 * positive[...], "dx", 4)
    far_wait()
    passage_term(1)
    rest_encode()
    rest_send()
    sib_send(1)
    query_term(0)
    finish = total_along(finish(), "dy", 4)
    passage_term(0)
    sib_send(0)
    add_sibling(3, 4)
    z_near(2, 0)
    near_add()
    z_near(2, 1)
    finish = total_along(finish(), "dz", 8)
    add_sibling(1, 2, 0)
    rest_add(0)
    last_send(3, 1)
    z_near(1, 0)
    rest_add(1)
    last_send(2)
    z_near(1, 1)
    finish = total_along(finish(), "dc", 2)
    total = finish()
    loss_out[...] = jnp.sum(jnp.sum(total, axis=1, keepdims=True), axis=0, keepdims=True) * (LN2 / (2.0 * PAIRS))
    query_out()
    passage_out()
    for copy in sent:
        copy.wait_send()


def on_device(queries, passages, pair):
    vmem = pl.BlockSpec(memory_space=pltpu.VMEM)
    anywhere = pl.BlockSpec(memory_space=pl.ANY)
    query_grad, passage_grad, loss = pl.pallas_call(
        kernel,
        out_shape=(
            pltpu.VMEM((OWN, D), bf16),
            pltpu.VMEM((OWN, D), bf16),
            jax.ShapeDtypeStruct((1, 1), f32),
        ),
        in_specs=[anywhere] * 3,
        out_specs=[vmem] * 3,
        scratch_shapes=[
            pltpu.VMEM((ROWS, D), bf16),
            pltpu.VMEM((ROWS, D), bf16),
            pltpu.VMEM((1, OWN), jnp.int32),
            pltpu.VMEM((ROWS, ROWS), f32),
            pltpu.VMEM((ROWS, ROWS), bf16),
            pltpu.VMEM((ROWS, 128), f32),
            pltpu.VMEM((ROWS, 128), f32),
            pltpu.VMEM((8, ROWS), f32),
            pltpu.VMEM((8, ROWS), f32),
            pltpu.VMEM((16, 40, 128), f32),
            pltpu.VMEM((16, 16, 128), f32),
            pltpu.VMEM((32, 128), f32),
            pltpu.VMEM((ROWS, 128), f32),
            pltpu.VMEM((ROWS, 128), f32),
            pltpu.VMEM((128, 128), f32),
            pltpu.VMEM((16, 128), f32),
            pltpu.VMEM((1, ROWS), f32),
            pltpu.VMEM((1, ROWS), f32),
            pltpu.VMEM((ROWS, D), f32),
            pltpu.VMEM((ROWS // 2, D), f32),
            pltpu.VMEM((2, 2, tiles(OWN, D), 16, 128), i16),
            pltpu.VMEM((2, 2, tiles(OWN, D), 16, 128), i16),
            pltpu.VMEM((2, 2, tiles(OWN, D), 16, 128), i16),
            pltpu.VMEM((2, 2, tiles(OWN, D), 16, 128), i16),
            pltpu.VMEM((2, 2, 2, tiles(HALF, D), 16, 128), i16),
            pltpu.VMEM((2, 2, 2, tiles(HALF, D), 16, 128), i16),
            pltpu.VMEM((2, 3, tiles(HALF, D), 16, 128), i16),
            pltpu.VMEM((2, 3, tiles(HALF, D), 16, 128), i16),
            pltpu.VMEM((2, tiles(HALF, D), 16, 128), i16),
            pltpu.VMEM((2, tiles(HALF, D), 16, 128), i16),
            pltpu.VMEM((3, 2, 2, tiles(HALF, D), 16, 128), i16),
            pltpu.VMEM((3, 2, 2, tiles(HALF, D), 16, 128), i16),
            pltpu.VMEM((18, 8, 128), f32),
            pltpu.VMEM((18, 8, 128), f32),
            pltpu.VMEM((8, 128), f32),
            pltpu.SemaphoreType.DMA((MESSAGES,)),
            pltpu.SemaphoreType.DMA((MESSAGES,)),
            pltpu.SemaphoreType.DMA((4,)),
        ],
        compiler_params=pltpu.CompilerParams(
            collective_id=0, has_side_effects=True, vmem_limit_bytes=60 * 1024 * 1024
        ),
    )(queries, passages, pair.reshape(1, OWN))
    return query_grad, passage_grad, loss.reshape(())


def solution(mesh):
    in_specs = (P(("loop", "grp"), None), P(("grp", "loop"), None), P(("loop", "grp")))
    out_specs = (P(("loop", "grp"), None), P(("grp", "loop"), None), P())
    return jax.shard_map(
        on_device, mesh=mesh, in_specs=in_specs, out_specs=out_specs, check_vma=False
    )
```

```python
import functools
import math

import jax
import jax.numpy as jnp
from jax import lax
from jax.experimental import pallas as pl
from jax.experimental.pallas import tpu as pltpu
from jax.sharding import PartitionSpec as P

MESH = pl.DeviceIdType.MESH
D = 1024
OWN = 96
HALF = 48
ROWS = 1536
BUNDLE = 192
CHUNK = 384
COLS = 512
PAIRS = 24576
TO_LOG2 = 50.0 * math.log2(math.e)
LN2 = math.log(2.0)
GRAD_SCALE = 25.0
LEVELS = 32000.0
SMALLEST = 1e-30
LOWEST = -1e38
RING4 = (0, 1, -1, 2)
RING8 = (0, 1, -1, 2, -2, 3, -3, 4)
AT4 = {0: 0, 1: 1, -1: 2, 2: 3}
AT8 = {0: 0, 1: 1, -1: 2, 2: 3, -2: 4, 3: 5, -3: 6, 4: 7}
MESSAGES = 144
f32 = jnp.float32
bf16 = jnp.bfloat16
i16 = jnp.int16


def tiles(rows, cols):
    return (rows // 16) * (cols // 128) + 1


def kernel(
    q_in, p_in, pair_in, qg_out, pg_out, loss_out,
    q_all, p_all, pair_own, scores, w,
    row_peak, row_sum, col_peak, col_sum,
    row_stats, col_stats, row_lse, row_rep, pair_rep, order, col_lse, col_rep, col_index,
    term, sib, far_out, far_in, near_out, near_in, rest_out, rest_in, last_out, last_in,
    z_far_out, z_far_in, z_out, z_in, loss_out_buf, loss_in_buf, positive,
    send_sem, recv_sem, own_sem,
):
    loop = lax.axis_index("loop")
    grp = lax.axis_index("grp")
    core = lax.rem(grp, 2)
    x = lax.rem(lax.div(grp, 2), 4)
    y = lax.div(loop, 8) * 2 + lax.div(grp, 8)
    z = lax.rem(loop, 8)

    xs = [x] + [lax.rem(x + d, 4) for d in (1, 2, 3)]
    ys = [y] + [lax.rem(y + d, 4) for d in (1, 2, 3)]
    zs8 = [z] + [lax.rem(z + d, 8) for d in range(1, 8)]
    cores = [core, 1 - core]
    y_loop = [lax.div(v, 2) * 8 for v in ys]
    y_grp = [lax.rem(v, 2) * 8 for v in ys]

    def device(dx=0, dy=0, dz=0, dc=0):
        return {
            "loop": y_loop[dy % 4] + zs8[dz % 8],
            "grp": y_grp[dy % 4] + xs[dx % 4] * 2 + cores[dc],
        }

    def hops(d, size):
        return min(d, size - d)

    plane = [(dx, dy) for dx in range(4) for dy in range(4) if dx or dy]
    plane.sort(key=lambda d: -hops(d[0], 4) - hops(d[1], 4))
    column = [(dz, dc) for dz in range(8) for dc in range(2) if dz or dc]
    column.sort(key=lambda d: -hops(d[0], 8) * 2 - d[1])

    barrier = pltpu.get_barrier_semaphore()
    neighbours = [{"dx": 1}, {"dx": -1}, {"dy": 1}, {"dy": -1}, {"dz": 1}, {"dz": -1}, {"dc": 1}]
    for where in neighbours:
        pl.semaphore_signal(barrier, inc=1, device_id=device(**where), device_id_type=MESH)
    own = [
        pltpu.make_async_copy(src, dst, own_sem.at[k])
        for k, (src, dst) in enumerate(
            (
                (q_in.at[pl.ds(0, HALF), :], q_all.at[pl.ds(0, HALF), :]),
                (q_in.at[pl.ds(HALF, HALF), :], q_all.at[pl.ds(BUNDLE, HALF), :]),
                (p_in, p_all.at[pl.ds(0, OWN), :]),
                (pair_in, pair_own),
            )
        )
    ]
    for copy in own:
        copy.start()

    count = [0]
    sent = []

    def send(src, dst, **where):
        k = count[0]
        count[0] += 1
        copy = pltpu.make_async_remote_copy(
            src_ref=src, dst_ref=dst, send_sem=send_sem.at[k], recv_sem=recv_sem.at[k],
            device_id=device(**where), device_id_type=MESH,
        )
        copy.start()
        sent.append(copy)
        return copy

    def q_at(half, p, q, cols=(0, D)):
        return q_all.at[pl.ds((2 * p + half) * BUNDLE + q * HALF, HALF), pl.ds(*cols)]

    def p_at(pos, rel, h=None):
        start = pos * BUNDLE + rel * OWN
        if h is None:
            return p_all.at[pl.ds(start, OWN), :]
        return p_all.at[pl.ds(start + h * HALF, HALF), :]

    pl.semaphore_wait(barrier, len(neighbours))
    for copy in own:
        copy.wait()

    first_axis, second_axis = ("dx", "dy"), ("dy", "dx")
    zs, near1, far1, near2, far2, sibling = {}, {}, {}, {}, {}, {}

    def spread(half, q):
        for sign in (1, -1):
            near2[half, sign, q] = send(
                q_at(half, 0, q), q_at(half, AT4[-sign], q), **{second_axis[half]: sign}
            )

    def z_own(h):
        for sign in (1, -1):
            zs[sign, 1, h] = send(p_at(0, 0, h), p_at(AT8[-sign], 0, h), dz=sign)

    def z_pass(k, h):
        for sign in (1, -1):
            last = h != (0 if sign == 1 else 1)
            if k == 4 and last:
                continue
            zs[sign, k, h].wait_recv()
            if k < 3 or (k == 3 and not last):
                pos, to = AT8[-sign * k], AT8[-sign * (k + 1)] if k < 3 else 7
                zs[sign, k + 1, h] = send(p_at(pos, 0, h), p_at(to, 0, h), dz=sign)

    def to_sibling(*positions):
        for pos in positions:
            sibling[pos] = send(p_at(pos, 0), p_at(pos, 1), dc=1)

    def pass_far(q):
        for half in (0, 1):
            for sign in (1, -1):
                near2[half, sign, q].wait_recv()
                if (q < 2) == (sign == 1):
                    far2[half, q] = send(
                        q_at(half, AT4[-sign], q), q_at(half, 3, q), **{second_axis[half]: sign}
                    )

    for half in (0, 1):
        for sign in (1, -1):
            near1[half, sign] = send(q_at(half, 0, 0), q_at(half, 0, AT4[-sign]), **{first_axis[half]: sign})
    z_own(0)
    for half in (0, 1):
        spread(half, 0)
    z_own(1)
    to_sibling(0)
    row_peak[...] = jnp.full(row_peak.shape, LOWEST, f32)
    row_sum[...] = jnp.zeros(row_sum.shape, f32)
    col_peak[...] = jnp.full(col_peak.shape, LOWEST, f32)
    col_sum[...] = jnp.zeros(col_sum.shape, f32)
    slot = x * 4 + y
    col_slot = z * 2 + core
    row_stats[slot] = jnp.zeros((40, 128), f32)
    col_stats[col_slot] = jnp.zeros((16, 128), f32)
    row_stats[slot, pl.ds(32, 1), pl.ds(0, OWN)] = pair_own[...].astype(f32)

    z_pass(1, 0)
    for half in (0, 1):
        for sign in (1, -1):
            q = AT4[-sign]
            near1[half, sign].wait_recv()
            cols = (0, D // 2) if sign == 1 else (D // 2, D // 2)
            far1[half, sign] = send(q_at(half, 0, q, cols), q_at(half, 0, 3, cols), **{first_axis[half]: sign})
            spread(half, q)
    z_pass(1, 1)
    to_sibling(1, 2)
    pass_far(0)
    for half in (0, 1):
        for sign in (1, -1):
            far1[half, sign].wait_recv()
        spread(half, 3)
    z_pass(2, 0)

    def block(p, start, width):
        rows = pl.ds(p * CHUNK, CHUNK)
        cols = pl.ds(start, width)
        s = lax.dot_general(
            q_all[rows, :], p_all[cols, :], (((1,), (1,)), ((), ())), preferred_element_type=f32
        ) * TO_LOG2
        scores[rows, cols] = s
        parts = [s[:, 128 * i : 128 * (i + 1)] for i in range(width // 128)]
        old = row_peak[rows, :]
        peak = functools.reduce(jnp.maximum, parts, old)
        total = row_sum[rows, :] * jnp.exp2(old - peak)
        for part in parts:
            total += jnp.exp2(part - peak)
        row_peak[rows, :] = peak
        row_sum[rows, :] = total
        s3 = s.reshape(CHUNK // 8, 8, width)
        old = col_peak[:, cols]
        peak = jnp.maximum(old, jnp.max(s3, axis=0))
        col_sum[:, cols] = col_sum[:, cols] * jnp.exp2(old - peak) + jnp.sum(jnp.exp2(s3 - peak[None]), axis=0)
        col_peak[:, cols] = peak

    for pos in (0, 1, 2):
        sibling[pos].wait_recv()
    block(0, 0, 512)
    pass_far(1)
    z_pass(2, 1)
    to_sibling(3, 4)
    pass_far(2)
    z_pass(3, 0)
    pass_far(3)
    block(1, 0, 512)
    z_pass(3, 1)
    to_sibling(5, 6)
    block(2, 0, 512)
    for pos in (3, 4, 5, 6):
        sibling[pos].wait_recv()
    block(0, 512, 512)
    z_pass(4, 0)
    z_pass(4, 1)
    to_sibling(7)
    block(1, 512, 512)
    block(2, 512, 512)
    for half in (0, 1):
        for q in range(4):
            far2[half, q].wait_recv()
    block(3, 0, 1024)
    sibling[7].wait_recv()

    def piece(half, p, q):
        dx, dy = (RING4[q], RING4[p]) if half == 0 else (RING4[p], RING4[q])
        return xs[dx % 4] * 4 + ys[dy % 4]

    def owner(pos, rel):
        return zs8[RING8[pos] % 8] * 2 + cores[rel]

    def finish_rows(p):
        rows = pl.ds(p * CHUNK, CHUNK)
        lanes = row_peak[rows, :].T
        peak = jnp.max(lanes, axis=0, keepdims=True)
        total = jnp.sum(row_sum[rows, :].T * jnp.exp2(lanes - peak), axis=0, keepdims=True)
        lse = peak + jnp.log(total) * (1.0 / LN2)
        for half in (0, 1):
            for q in range(4):
                start = half * BUNDLE + q * HALF
                row_stats[slot, pl.ds(half * 16 + piece(half, p, q), 1), pl.ds(0, HALF)] = lse[:, start : start + HALF]

    block(0, 1024, 512)
    block(1, 1024, 512)
    finish_rows(0)
    block(2, 1024, 512)
    finish_rows(1)
    block(3, 1024, 512)
    finish_rows(2)
    peak = jnp.max(col_peak[...], axis=0, keepdims=True)
    total = jnp.sum(col_sum[...] * jnp.exp2(col_peak[...] - peak), axis=0, keepdims=True)
    lse = peak + jnp.log(total) * (1.0 / LN2)
    for pos in range(8):
        for rel in (0, 1):
            start = pos * BUNDLE + rel * OWN
            col_stats[col_slot, pl.ds(owner(pos, rel), 1), pl.ds(0, OWN)] = lse[:, start : start + OWN]
    finish_rows(3)
    row_msgs, col_msgs = [], []
    for (dx, dy), (dz, dc) in zip(plane, column, strict=True):
        row_msgs.append(send(row_stats.at[slot], row_stats.at[slot], dx=dx, dy=dy))
        col_msgs.append(send(col_stats.at[col_slot], col_stats.at[col_slot], dz=dz, dc=dc))

    j = lax.broadcasted_iota(jnp.int32, (1, ROWS), 1)
    part = lax.shift_right_logical(j * 683, 16)
    within = j - part * OWN
    pos = lax.shift_right_logical(part, 1)
    away = lax.shift_right_logical(pos + 1, 1)
    away = jnp.where((pos & 1) == 1, away, -away)
    z2 = (z + away + 8) & 7
    c2 = (core + part) & 1
    first = (lax.div(grp, 2) * 2 + c2) * 16 + lax.div(loop, 8) * 8 + z2
    col_index[...] = (first * OWN + within).astype(f32)

    for m in row_msgs:
        m.wait_recv()
    stats = row_stats[:, 0:32, :]
    peak = jnp.max(stats, axis=0)
    lse = peak + jnp.log(jnp.sum(jnp.exp2(stats - peak[None]), axis=0)) * (1.0 / LN2)
    row_lse[...] = lse
    lane = lax.broadcasted_iota(jnp.int32, (32, 128), 1)
    share = jnp.sum(jnp.where(lane < HALF, lse, 0.0).reshape(4, 8, 128), axis=0)
    order[pl.ds(64, 64), :] = jnp.zeros((64, 128), f32)
    for b in range(8):
        p, half = b // 2, b % 2
        for q in range(4):
            at = piece(half, p, q)
            order[pl.ds(4 * b + q, 1), :] = row_lse[pl.ds(half * 16 + at, 1), :]
            order[pl.ds(32 + 4 * b + q, 1), :] = row_stats[at, pl.ds(32, 1), :]
    turned = order[...].T
    for b in range(8):
        half = b % 2
        for q in range(4):
            n = 4 * b + q
            rows = pl.ds(n * HALF, HALF)
            row_rep[rows, :] = jnp.broadcast_to(turned[0:HALF, n : n + 1], (HALF, 128))
            pair_rep[rows, :] = jnp.broadcast_to(
                turned[half * HALF : (half + 1) * HALF, 32 + n : 33 + n], (HALF, 128)
            )

    for m in col_msgs:
        m.wait_recv()
    stats = col_stats[...]
    peak = jnp.max(stats, axis=0)
    lse = peak + jnp.log(jnp.sum(jnp.exp2(stats - peak[None]), axis=0)) * (1.0 / LN2)
    col_lse[...] = lse
    lane = lax.broadcasted_iota(jnp.int32, (16, 128), 1)
    share = share + jnp.sum(jnp.where(lane < OWN, lse, 0.0).reshape(2, 8, 128), axis=0)
    col_rep[...] = jnp.concatenate(
        [col_lse[pl.ds(owner(pos, rel), 1), :][:, 0:OWN] for pos in range(8) for rel in (0, 1)], axis=1
    )

    positive[...] = jnp.zeros((8, 128), f32)

    def weigh(p, k):
        rows, cols = pl.ds(p * CHUNK, CHUNK), pl.ds(k * CHUNK, CHUNK)
        s = scores[rows, cols]
        hit = jnp.concatenate([pair_rep[rows, :]] * 3, axis=1) == col_index[:, cols]
        weight = (
            jnp.exp2(s - jnp.concatenate([row_rep[rows, :]] * 3, axis=1))
            + jnp.exp2(s - col_rep[:, cols])
            - jnp.where(hit, 2.0, 0.0)
        )
        found = jnp.sum(jnp.where(hit, s, 0.0).reshape(CHUNK // 8, 8, CHUNK), axis=0)
        positive[...] += found[:, 0:128] + found[:, 128:256] + found[:, 256:384]
        w[rows, cols] = weight.astype(bf16)

    def query_term(p):
        rows = pl.ds(p * CHUNK, CHUNK)
        scores[rows, pl.ds(0, D)] = jnp.dot(w[rows, :], p_all[...], preferred_element_type=f32)

    def near_rows(half, s, side):
        return (1 + s) * CHUNK + half * BUNDLE + side * OWN

    def near_terms(part):
        starts = [near_rows(half, s, s if part else 1 - s) for half in (0, 1) for s in (0, 1)]
        rows = jnp.concatenate([w[pl.ds(start, OWN), :] for start in starts], axis=0)
        out = jnp.dot(rows, p_all[...], preferred_element_type=f32)
        for i, start in enumerate(starts):
            scores[pl.ds(start, OWN), pl.ds(0, D)] = out[i * OWN : (i + 1) * OWN, :]

    sib_msgs = {}

    def passage_term(k):
        rows = pl.ds(k * CHUNK, CHUNK)
        term[rows, :] = lax.dot_general(
            w[:, rows], q_all[...], (((0,), (0,)), ((), ())), preferred_element_type=f32
        )

    def sib_send(k):
        for pos in (2 * k + 1, 2 * k):
            sib_msgs[pos] = send(
                term.at[pl.ds(pos * BUNDLE + OWN, OWN), :], sib.at[pl.ds(pos * OWN, OWN), :], dc=1
            )

    def add_sibling(*positions):
        for pos in positions:
            sib_msgs[pos].wait_recv()
        for pos in positions:
            term[pl.ds(pos * BUNDLE, OWN), :] += sib[pl.ds(pos * OWN, OWN), :]

    def encode(ref, r0, rows, c0, cols, buf):
        peak = functools.reduce(
            jnp.maximum,
            [
                jnp.max(jnp.abs(ref[pl.ds(r0, rows), pl.ds(c0 + 128 * i, 128)]).reshape(rows // 8, 8, 128), axis=0)
                for i in range(cols // 128)
            ],
        )
        power = jnp.floor(jnp.log(jnp.maximum(peak, SMALLEST)) * (1.0 / LN2)) + 1.0
        factor = (jnp.exp2(-power) * LEVELS)[None]
        n = rows // 16
        for i in range(cols // 128):
            v = ref[pl.ds(r0, rows), pl.ds(c0 + 128 * i, 128)].reshape(rows // 8, 8, 128) * factor
            buf[pl.ds(i * n, n)] = jnp.round(v).astype(jnp.int32).reshape(n, 16, 128).astype(i16)
        both = jnp.concatenate([power, power], axis=0).astype(jnp.int32)
        buf[pl.ds(n * (cols // 128), 1)] = both.astype(i16)[None]

    def add_decoded(ref, r0, rows, c0, cols, buf):
        n = rows // 16
        power = buf[n * (cols // 128)].astype(jnp.int32).astype(f32)[0:8]
        factor = (jnp.exp2(power) * (1.0 / LEVELS))[None]
        for i in range(cols // 128):
            v = buf[pl.ds(i * n, n)].astype(jnp.int32).astype(f32).reshape(rows // 8, 8, 128) * factor
            ref[pl.ds(r0, rows), pl.ds(c0 + 128 * i, 128)] += v.reshape(rows, 128)

    msgs = {}
    sides = [(half, sign, s) for half in (0, 1) for sign, s in ((1, 0), (-1, 1))]

    def far_send():
        for half, _, s in sides:
            encode(scores, 3 * CHUNK + half * BUNDLE + s * OWN, OWN, 0, D, far_out.at[half, s])
        for half, sign, s in sides:
            msgs["far", half, s] = send(far_out.at[half, s], far_in.at[half, s], **{second_axis[half]: sign})

    def near_send():
        for half, _, s in sides:
            encode(scores, near_rows(half, s, 1 - s), OWN, 0, D, near_out.at[half, s])
        for half, sign, s in sides:
            msgs["near", half, s] = send(near_out.at[half, s], near_in.at[half, s], **{second_axis[half]: sign})

    def far_wait():
        for half, _, s in sides:
            msgs["far", half, s].wait_recv()

    def rest_encode():
        for half, _, s in sides:
            row = near_rows(half, s, s)
            add_decoded(scores, row, OWN, 0, D, far_in.at[half, s])
            for u in (0, 1):
                encode(scores, row + (1 - u) * HALF, HALF, 0, D, rest_out.at[half, s, u])

    def rest_send():
        for u in (0, 1):
            for half, sign, s in sides:
                msgs["rest", half, s, u] = send(
                    rest_out.at[half, s, u], rest_in.at[half, s, u], **{second_axis[half]: sign}
                )

    def near_add():
        for half, _, s in sides:
            msgs["near", half, s].wait_recv()
        for half, _, s in sides:
            add_decoded(scores, half * BUNDLE + (1 - s) * OWN, OWN, 0, D, near_in.at[half, s])

    def rest_add(u):
        for half, _, s in sides:
            msgs["rest", half, s, u].wait_recv()
        for half, _, s in sides:
            add_decoded(scores, half * BUNDLE + s * OWN + (1 - u) * HALF, HALF, 0, D, rest_in.at[half, s, u])

    def last_send(*qs):
        for half in (0, 1):
            for q in qs:
                encode(scores, half * BUNDLE + q * HALF, HALF, 0, D, last_out.at[half, q - 1])
        for q in qs:
            for half in (0, 1):
                msgs["last", half, q] = send(
                    last_out.at[half, q - 1], last_in.at[half, q - 1], **{first_axis[half]: RING4[q]}
                )

    def query_out():
        for q in (1, 3, 2):
            for half in (0, 1):
                msgs["last", half, q].wait_recv()
            for half in (0, 1):
                add_decoded(scores, half * BUNDLE, HALF, 0, D, last_in.at[half, q - 1])
        for half in (0, 1):
            rows = pl.ds(half * BUNDLE, HALF)
            qg_out[pl.ds(half * HALF, HALF), :] = (scores[rows, pl.ds(0, D)] * GRAD_SCALE).astype(bf16)

    def z_far():
        for s in (0, 1):
            encode(term, 7 * BUNDLE + s * HALF, HALF, 0, D, z_far_out.at[s])
        for sign, s in ((1, 0), (-1, 1)):
            msgs["z", 4, s] = send(z_far_out.at[s], z_far_in.at[s], dz=sign)

    def z_near(k, part):
        rows = [AT8[sign * k] * BUNDLE + (s if part else 1 - s) * HALF for sign, s in ((1, 0), (-1, 1))]
        if k < 3:
            arrived = [(msgs["z", k + 1, s, part], z_in.at[k, s, part]) for s in (0, 1)]
        else:
            arrived = [(msgs["z", 4, s], z_far_in.at[s]) for s in (0, 1)] if part else []
        for message, _ in arrived:
            message.wait_recv()
        for row, (_, buf) in zip(rows, arrived):
            add_decoded(term, row, HALF, 0, D, buf)
        for s in (0, 1):
            encode(term, rows[s], HALF, 0, D, z_out.at[k - 1, s, part])
        for sign, s in ((1, 0), (-1, 1)):
            msgs["z", k, s, part] = send(z_out.at[k - 1, s, part], z_in.at[k - 1, s, part], dz=sign)

    def passage_out():
        for part in (0, 1):
            for s in (0, 1):
                msgs["z", 1, s, part].wait_recv()
            for s in (0, 1):
                add_decoded(term, (s if part else 1 - s) * HALF, HALF, 0, D, z_in.at[0, s, part])
        pg_out[...] = (term[pl.ds(0, OWN), :] * GRAD_SCALE).astype(bf16)

    loss_slot = [0]

    def total_along(value, axis, size):
        base = loss_slot[0]
        loss_slot[0] += size
        loss_out_buf[base] = value
        copies = [
            send(loss_out_buf.at[base], loss_in_buf.at[base + d], **{axis: d}) for d in range(1, size)
        ]

        def finish():
            out = value
            for d, m in enumerate(copies, 1):
                m.wait_recv()
                out = out + loss_in_buf[base + d]
            return out

        return finish

    for p in range(4):
        weigh(p, 3)
    passage_term(3)
    for k in range(3):
        weigh(3, k)
    sib_send(3)
    query_term(3)
    for p in range(3):
        weigh(p, 2)
    far_send()
    add_sibling(7)
    z_far()
    passage_term(2)
    for p in (1, 2):
        for k in (0, 1):
            weigh(p, k)
    sib_send(2)
    near_terms(0)
    for k in (0, 1):
        weigh(0, k)
    near_send()
    add_sibling(5, 6)
    z_near(3, 0)
    z_near(3, 1)
    finish = total_along(share * (1.0 / 16.0) - 2.0 * positive[...], "dx", 4)
    passage_term(1)
    sib_send(1)
    near_terms(1)
    far_wait()
    rest_encode()
    rest_send()
    add_sibling(3, 4)
    z_near(2, 0)
    finish = total_along(finish(), "dy", 4)
    passage_term(0)
    sib_send(0)
    z_near(2, 1)
    query_term(0)
    near_add()
    rest_add(0)
    last_send(3, 1)
    finish = total_along(finish(), "dz", 8)
    add_sibling(1, 2, 0)
    z_near(1, 0)
    rest_add(1)
    last_send(2)
    z_near(1, 1)
    finish = total_along(finish(), "dc", 2)
    total = finish()
    loss_out[...] = jnp.sum(jnp.sum(total, axis=1, keepdims=True), axis=0, keepdims=True) * (LN2 / (2.0 * PAIRS))
    query_out()
    passage_out()
    for copy in sent:
        copy.wait_send()


def on_device(queries, passages, pair):
    vmem = pl.BlockSpec(memory_space=pltpu.VMEM)
    anywhere = pl.BlockSpec(memory_space=pl.ANY)
    query_grad, passage_grad, loss = pl.pallas_call(
        kernel,
        out_shape=(
            pltpu.VMEM((OWN, D), bf16),
            pltpu.VMEM((OWN, D), bf16),
            jax.ShapeDtypeStruct((1, 1), f32),
        ),
        in_specs=[anywhere] * 3,
        out_specs=[vmem] * 3,
        scratch_shapes=[
            pltpu.VMEM((ROWS, D), bf16),
            pltpu.VMEM((ROWS, D), bf16),
            pltpu.VMEM((1, OWN), jnp.int32),
            pltpu.VMEM((ROWS, ROWS), f32),
            pltpu.VMEM((ROWS, ROWS), bf16),
            pltpu.VMEM((ROWS, 128), f32),
            pltpu.VMEM((ROWS, 128), f32),
            pltpu.VMEM((8, ROWS), f32),
            pltpu.VMEM((8, ROWS), f32),
            pltpu.VMEM((16, 40, 128), f32),
            pltpu.VMEM((16, 16, 128), f32),
            pltpu.VMEM((32, 128), f32),
            pltpu.VMEM((ROWS, 128), f32),
            pltpu.VMEM((ROWS, 128), f32),
            pltpu.VMEM((128, 128), f32),
            pltpu.VMEM((16, 128), f32),
            pltpu.VMEM((1, ROWS), f32),
            pltpu.VMEM((1, ROWS), f32),
            pltpu.VMEM((ROWS, D), f32),
            pltpu.VMEM((ROWS // 2, D), f32),
            pltpu.VMEM((2, 2, tiles(OWN, D), 16, 128), i16),
            pltpu.VMEM((2, 2, tiles(OWN, D), 16, 128), i16),
            pltpu.VMEM((2, 2, tiles(OWN, D), 16, 128), i16),
            pltpu.VMEM((2, 2, tiles(OWN, D), 16, 128), i16),
            pltpu.VMEM((2, 2, 2, tiles(HALF, D), 16, 128), i16),
            pltpu.VMEM((2, 2, 2, tiles(HALF, D), 16, 128), i16),
            pltpu.VMEM((2, 3, tiles(HALF, D), 16, 128), i16),
            pltpu.VMEM((2, 3, tiles(HALF, D), 16, 128), i16),
            pltpu.VMEM((2, tiles(HALF, D), 16, 128), i16),
            pltpu.VMEM((2, tiles(HALF, D), 16, 128), i16),
            pltpu.VMEM((3, 2, 2, tiles(HALF, D), 16, 128), i16),
            pltpu.VMEM((3, 2, 2, tiles(HALF, D), 16, 128), i16),
            pltpu.VMEM((18, 8, 128), f32),
            pltpu.VMEM((18, 8, 128), f32),
            pltpu.VMEM((8, 128), f32),
            pltpu.SemaphoreType.DMA((MESSAGES,)),
            pltpu.SemaphoreType.DMA((MESSAGES,)),
            pltpu.SemaphoreType.DMA((4,)),
        ],
        compiler_params=pltpu.CompilerParams(
            collective_id=0, has_side_effects=True, vmem_limit_bytes=60 * 1024 * 1024
        ),
    )(queries, passages, pair.reshape(1, OWN))
    return query_grad, passage_grad, loss.reshape(())


def solution(mesh):
    in_specs = (P(("loop", "grp"), None), P(("grp", "loop"), None), P(("loop", "grp")))
    out_specs = (P(("loop", "grp"), None), P(("grp", "loop"), None), P())
    return jax.shard_map(
        on_device, mesh=mesh, in_specs=in_specs, out_specs=out_specs, check_vma=False
    )
```

```python
import functools
import math

import jax
import jax.numpy as jnp
from jax import lax
from jax.experimental import pallas as pl
from jax.experimental.pallas import tpu as pltpu
from jax.sharding import PartitionSpec as P

MESH = pl.DeviceIdType.MESH
D = 1024
OWN = 96
HALF = 48
ROWS = 1536
BUNDLE = 192
CHUNK = 384
COLS = 512
PAIRS = 24576
TO_LOG2 = 50.0 * math.log2(math.e)
LN2 = math.log(2.0)
GRAD_SCALE = 25.0
LEVELS = 32000.0
SMALLEST = 1e-30
LOWEST = -1e38
RING4 = (0, 1, -1, 2)
RING8 = (0, 1, -1, 2, -2, 3, -3, 4)
AT4 = {0: 0, 1: 1, -1: 2, 2: 3}
AT8 = {0: 0, 1: 1, -1: 2, 2: 3, -2: 4, 3: 5, -3: 6, 4: 7}
MESSAGES = 144
f32 = jnp.float32
bf16 = jnp.bfloat16
i16 = jnp.int16


def tiles(rows, cols):
    return (rows // 16) * (cols // 128) + 1


def kernel(
    q_in, p_in, pair_in, qg_out, pg_out, loss_out,
    q_all, p_all, pair_own, scores, w,
    row_peak, row_sum, col_peak, col_sum,
    row_stats, col_stats, row_lse, pair_all, row_rep, pair_rep, order, col_lse, col_rep, col_index,
    term, sib, far_out, far_in, near_out, near_in, rest_out, rest_in, last_out, last_in,
    z_far_out, z_far_in, z_out, z_in, loss_out_buf, loss_in_buf, positive,
    send_sem, recv_sem, own_sem,
):
    loop = lax.axis_index("loop")
    grp = lax.axis_index("grp")
    core = lax.rem(grp, 2)
    x = lax.rem(lax.div(grp, 2), 4)
    y = lax.div(loop, 8) * 2 + lax.div(grp, 8)
    z = lax.rem(loop, 8)

    xs = [x] + [lax.rem(x + d, 4) for d in (1, 2, 3)]
    ys = [y] + [lax.rem(y + d, 4) for d in (1, 2, 3)]
    zs8 = [z] + [lax.rem(z + d, 8) for d in range(1, 8)]
    cores = [core, 1 - core]
    y_loop = [lax.div(v, 2) * 8 for v in ys]
    y_grp = [lax.rem(v, 2) * 8 for v in ys]

    def device(dx=0, dy=0, dz=0, dc=0):
        return {
            "loop": y_loop[dy % 4] + zs8[dz % 8],
            "grp": y_grp[dy % 4] + xs[dx % 4] * 2 + cores[dc],
        }

    def hops(d, size):
        return min(d, size - d)

    plane = [(dx, dy) for dx in range(4) for dy in range(4) if dx or dy]
    plane.sort(key=lambda d: -hops(d[0], 4) - hops(d[1], 4))
    column = [(dz, dc) for dz in range(8) for dc in range(2) if dz or dc]
    column.sort(key=lambda d: -hops(d[0], 8) * 2 - d[1])

    barrier = pltpu.get_barrier_semaphore()
    neighbours = [{"dx": 1}, {"dx": -1}, {"dy": 1}, {"dy": -1}, {"dz": 1}, {"dz": -1}, {"dc": 1}]
    neighbours += [{"dx": 2}, {"dy": 2}]
    for where in neighbours:
        pl.semaphore_signal(barrier, inc=1, device_id=device(**where), device_id_type=MESH)
    own = [
        pltpu.make_async_copy(src, dst, own_sem.at[k])
        for k, (src, dst) in enumerate(
            (
                (q_in.at[pl.ds(0, HALF), :], q_all.at[pl.ds(0, HALF), :]),
                (q_in.at[pl.ds(HALF, HALF), :], q_all.at[pl.ds(BUNDLE, HALF), :]),
                (p_in, p_all.at[pl.ds(0, OWN), :]),
                (pair_in, pair_own),
            )
        )
    ]
    for copy in own:
        copy.start()

    count = [0]
    sent = []

    def send(src, dst, **where):
        k = count[0]
        count[0] += 1
        copy = pltpu.make_async_remote_copy(
            src_ref=src, dst_ref=dst, send_sem=send_sem.at[k], recv_sem=recv_sem.at[k],
            device_id=device(**where), device_id_type=MESH,
        )
        copy.start()
        sent.append(copy)
        return copy

    def q_at(half, p, q):
        return q_all.at[pl.ds((2 * p + half) * BUNDLE + q * HALF, HALF), :]

    def p_at(pos, rel, h=None):
        start = pos * BUNDLE + rel * OWN
        if h is None:
            return p_all.at[pl.ds(start, OWN), :]
        return p_all.at[pl.ds(start + h * HALF, HALF), :]

    pl.semaphore_wait(barrier, len(neighbours))
    for copy in own:
        copy.wait()

    first_axis, second_axis = ("dx", "dy"), ("dy", "dx")
    zs, near1, far1, near2, far2, sibling = {}, {}, {}, {}, {}, {}

    def spread(half, q):
        for sign in (1, -1):
            near2[half, sign, q] = send(
                q_at(half, 0, q), q_at(half, AT4[-sign], q), **{second_axis[half]: sign}
            )

    def z_own(h):
        for sign in (1, -1):
            zs[sign, 1, h] = send(p_at(0, 0, h), p_at(AT8[-sign], 0, h), dz=sign)

    def z_pass(k, h):
        for sign in (1, -1):
            last = h != (0 if sign == 1 else 1)
            if k == 4 and last:
                continue
            zs[sign, k, h].wait_recv()
            if k < 3 or (k == 3 and not last):
                pos, to = AT8[-sign * k], AT8[-sign * (k + 1)] if k < 3 else 7
                zs[sign, k + 1, h] = send(p_at(pos, 0, h), p_at(to, 0, h), dz=sign)

    def to_sibling(*positions):
        for pos in positions:
            sibling[pos] = send(p_at(pos, 0), p_at(pos, 1), dc=1)

    def pass_far(q):
        for half in (0, 1):
            for sign in (1, -1):
                near2[half, sign, q].wait_recv()
                if (q < 2) == (sign == 1):
                    far2[half, q] = send(
                        q_at(half, AT4[-sign], q), q_at(half, 3, q), **{second_axis[half]: sign}
                    )

    for half in (0, 1):
        for sign in (1, -1):
            near1[half, sign] = send(q_at(half, 0, 0), q_at(half, 0, AT4[-sign]), **{first_axis[half]: sign})
    z_own(0)
    for half in (0, 1):
        far1[half] = send(q_at(half, 0, 0), q_at(half, 0, 3), **{first_axis[half]: 2})
    for half in (0, 1):
        spread(half, 0)
    z_own(1)
    to_sibling(0)
    row_peak[...] = jnp.full(row_peak.shape, LOWEST, f32)
    row_sum[...] = jnp.zeros(row_sum.shape, f32)
    col_peak[...] = jnp.full(col_peak.shape, LOWEST, f32)
    col_sum[...] = jnp.zeros(col_sum.shape, f32)
    slot = x * 4 + y
    col_slot = z * 2 + core
    row_stats[slot] = jnp.zeros((16, 128), f32)
    col_stats[col_slot] = jnp.zeros((16, 128), f32)
    for i in range(3):
        row_stats[slot, pl.ds(i, 1), pl.ds(OWN, 32)] = pair_own[:, 32 * i : 32 * (i + 1)].astype(f32)

    z_pass(1, 0)
    for half in (0, 1):
        for sign in (1, -1):
            near1[half, sign].wait_recv()
            spread(half, AT4[-sign])
    z_pass(1, 1)
    to_sibling(1, 2)
    pass_far(0)
    for half in (0, 1):
        far1[half].wait_recv()
        spread(half, 3)
    z_pass(2, 0)

    def block(p, start, width):
        rows = pl.ds(p * CHUNK, CHUNK)
        cols = pl.ds(start, width)
        s = lax.dot_general(
            q_all[rows, :], p_all[cols, :], (((1,), (1,)), ((), ())), preferred_element_type=f32
        ) * TO_LOG2
        scores[rows, cols] = s
        parts = [s[:, 128 * i : 128 * (i + 1)] for i in range(width // 128)]
        old = row_peak[rows, :]
        peak = functools.reduce(jnp.maximum, parts, old)
        total = row_sum[rows, :] * jnp.exp2(old - peak)
        for part in parts:
            total += jnp.exp2(part - peak)
        row_peak[rows, :] = peak
        row_sum[rows, :] = total
        s3 = s.reshape(CHUNK // 8, 8, width)
        old = col_peak[:, cols]
        peak = jnp.maximum(old, jnp.max(s3, axis=0))
        col_sum[:, cols] = col_sum[:, cols] * jnp.exp2(old - peak) + jnp.sum(jnp.exp2(s3 - peak[None]), axis=0)
        col_peak[:, cols] = peak

    for pos in (0, 1, 2):
        sibling[pos].wait_recv()
    block(0, 0, 512)
    pass_far(1)
    z_pass(2, 1)
    to_sibling(3, 4)
    pass_far(2)
    z_pass(3, 0)
    pass_far(3)
    block(1, 0, 512)
    z_pass(3, 1)
    to_sibling(5, 6)
    block(2, 0, 512)
    for pos in (3, 4, 5, 6):
        sibling[pos].wait_recv()
    block(0, 512, 512)
    z_pass(4, 0)
    z_pass(4, 1)
    to_sibling(7)
    block(1, 512, 512)
    block(2, 512, 512)
    for p in range(3):
        block(p, 1024, 256)
    for half in (0, 1):
        for q in range(4):
            far2[half, q].wait_recv()
    block(3, 0, 1280)
    sibling[7].wait_recv()

    def piece(half, p, q):
        dx, dy = (RING4[q], RING4[p]) if half == 0 else (RING4[p], RING4[q])
        return xs[dx % 4] * 4 + ys[dy % 4]

    def owner(pos, rel):
        return zs8[RING8[pos] % 8] * 2 + cores[rel]

    def finish_rows(p):
        rows = pl.ds(p * CHUNK, CHUNK)
        lanes = row_peak[rows, :].T
        peak = jnp.max(lanes, axis=0, keepdims=True)
        total = jnp.sum(row_sum[rows, :].T * jnp.exp2(lanes - peak), axis=0, keepdims=True)
        lse = peak + jnp.log(total) * (1.0 / LN2)
        for half in (0, 1):
            for q in range(4):
                start = half * BUNDLE + q * HALF
                row_stats[slot, pl.ds(piece(half, p, q), 1), pl.ds(half * HALF, HALF)] = lse[:, start : start + HALF]

    block(0, 1280, 256)
    block(1, 1280, 256)
    finish_rows(0)
    block(2, 1280, 256)
    finish_rows(1)
    block(3, 1280, 256)
    finish_rows(2)
    peak = jnp.max(col_peak[...], axis=0, keepdims=True)
    total = jnp.sum(col_sum[...] * jnp.exp2(col_peak[...] - peak), axis=0, keepdims=True)
    lse = peak + jnp.log(total) * (1.0 / LN2)
    for pos in range(8):
        for rel in (0, 1):
            start = pos * BUNDLE + rel * OWN
            col_stats[col_slot, pl.ds(owner(pos, rel), 1), pl.ds(0, OWN)] = lse[:, start : start + OWN]
    finish_rows(3)
    row_msgs, col_msgs = [], []
    for (dx, dy), (dz, dc) in zip(plane, column, strict=True):
        row_msgs.append(send(row_stats.at[slot], row_stats.at[slot], dx=dx, dy=dy))
        col_msgs.append(send(col_stats.at[col_slot], col_stats.at[col_slot], dz=dz, dc=dc))

    j = lax.broadcasted_iota(jnp.int32, (1, ROWS), 1)
    part = lax.shift_right_logical(j * 683, 16)
    within = j - part * OWN
    pos = lax.shift_right_logical(part, 1)
    away = lax.shift_right_logical(pos + 1, 1)
    away = jnp.where((pos & 1) == 1, away, -away)
    z2 = (z + away + 8) & 7
    c2 = (core + part) & 1
    first = (lax.div(grp, 2) * 2 + c2) * 16 + lax.div(loop, 8) * 8 + z2
    col_index[...] = (first * OWN + within).astype(f32)

    for m in row_msgs:
        m.wait_recv()
    stats = row_stats[...]
    lane = lax.broadcasted_iota(jnp.int32, (16, 128), 1)
    peak = jnp.max(stats, axis=0)
    lse = peak + jnp.log(jnp.sum(jnp.exp2(stats - peak[None]), axis=0)) * (1.0 / LN2)
    row_lse[...] = lse
    share = jnp.sum(jnp.where(lane < OWN, lse, 0.0).reshape(2, 8, 128), axis=0)
    for i in range(3):
        pair_all[:, pl.ds(32 * i, 32)] = stats[:, i, OWN:128]
    order[pl.ds(64, 64), :] = jnp.zeros((64, 128), f32)
    for b in range(8):
        p, half = b // 2, b % 2
        for q in range(4):
            at = piece(half, p, q)
            order[pl.ds(4 * b + q, 1), :] = row_lse[pl.ds(at, 1), :]
            order[pl.ds(32 + 4 * b + q, 1), :] = pair_all[pl.ds(at, 1), :]
    turned = order[...].T
    for b in range(8):
        half = b % 2
        for q in range(4):
            n = 4 * b + q
            rows = pl.ds(n * HALF, HALF)
            mine = turned[half * HALF : (half + 1) * HALF, :]
            row_rep[rows, :] = jnp.broadcast_to(mine[:, n : n + 1], (HALF, 128))
            pair_rep[rows, :] = jnp.broadcast_to(mine[:, 32 + n : 33 + n], (HALF, 128))

    for m in col_msgs:
        m.wait_recv()
    stats = col_stats[...]
    peak = jnp.max(stats, axis=0)
    lse = peak + jnp.log(jnp.sum(jnp.exp2(stats - peak[None]), axis=0)) * (1.0 / LN2)
    col_lse[...] = lse
    share = share + jnp.sum(jnp.where(lane < OWN, lse, 0.0).reshape(2, 8, 128), axis=0)
    col_rep[...] = jnp.concatenate(
        [col_lse[pl.ds(owner(pos, rel), 1), :][:, 0:OWN] for pos in range(8) for rel in (0, 1)], axis=1
    )

    positive[...] = jnp.zeros((8, 128), f32)

    def weigh(p, k):
        rows, cols = pl.ds(p * CHUNK, CHUNK), pl.ds(k * CHUNK, CHUNK)
        s = scores[rows, cols]
        hit = jnp.concatenate([pair_rep[rows, :]] * 3, axis=1) == col_index[:, cols]
        weight = (
            jnp.exp2(s - jnp.concatenate([row_rep[rows, :]] * 3, axis=1))
            + jnp.exp2(s - col_rep[:, cols])
            - jnp.where(hit, 2.0, 0.0)
        )
        found = jnp.sum(jnp.where(hit, s, 0.0).reshape(CHUNK // 8, 8, CHUNK), axis=0)
        positive[...] += found[:, 0:128] + found[:, 128:256] + found[:, 256:384]
        w[rows, cols] = weight.astype(bf16)

    def query_term(p):
        rows = pl.ds(p * CHUNK, CHUNK)
        scores[rows, pl.ds(0, D)] = jnp.dot(w[rows, :], p_all[...], preferred_element_type=f32)

    def near_rows(half, s, side):
        return (1 + s) * CHUNK + half * BUNDLE + side * OWN

    def near_terms(part):
        starts = [near_rows(half, s, s if part else 1 - s) for half in (0, 1) for s in (0, 1)]
        rows = jnp.concatenate([w[pl.ds(start, OWN), :] for start in starts], axis=0)
        out = jnp.dot(rows, p_all[...], preferred_element_type=f32)
        for i, start in enumerate(starts):
            scores[pl.ds(start, OWN), pl.ds(0, D)] = out[i * OWN : (i + 1) * OWN, :]

    sib_msgs = {}

    def passage_term(k):
        rows = pl.ds(k * CHUNK, CHUNK)
        term[rows, :] = lax.dot_general(
            w[:, rows], q_all[...], (((0,), (0,)), ((), ())), preferred_element_type=f32
        )

    def sib_send(k):
        for pos in (2 * k + 1, 2 * k):
            sib_msgs[pos] = send(
                term.at[pl.ds(pos * BUNDLE + OWN, OWN), :], sib.at[pl.ds(pos * OWN, OWN), :], dc=1
            )

    def add_sibling(*positions):
        for pos in positions:
            sib_msgs[pos].wait_recv()
        for pos in positions:
            term[pl.ds(pos * BUNDLE, OWN), :] += sib[pl.ds(pos * OWN, OWN), :]

    def encode(ref, r0, rows, c0, cols, buf):
        peak = functools.reduce(
            jnp.maximum,
            [
                jnp.max(jnp.abs(ref[pl.ds(r0, rows), pl.ds(c0 + 128 * i, 128)]).reshape(rows // 8, 8, 128), axis=0)
                for i in range(cols // 128)
            ],
        )
        power = jnp.floor(jnp.log(jnp.maximum(peak, SMALLEST)) * (1.0 / LN2)) + 1.0
        factor = (jnp.exp2(-power) * LEVELS)[None]
        n = rows // 16
        for i in range(cols // 128):
            v = ref[pl.ds(r0, rows), pl.ds(c0 + 128 * i, 128)].reshape(rows // 8, 8, 128) * factor
            buf[pl.ds(i * n, n)] = jnp.round(v).astype(jnp.int32).reshape(n, 16, 128).astype(i16)
        both = jnp.concatenate([power, power], axis=0).astype(jnp.int32)
        buf[pl.ds(n * (cols // 128), 1)] = both.astype(i16)[None]

    def add_decoded(ref, r0, rows, c0, cols, buf):
        n = rows // 16
        power = buf[n * (cols // 128)].astype(jnp.int32).astype(f32)[0:8]
        factor = (jnp.exp2(power) * (1.0 / LEVELS))[None]
        for i in range(cols // 128):
            v = buf[pl.ds(i * n, n)].astype(jnp.int32).astype(f32).reshape(rows // 8, 8, 128) * factor
            ref[pl.ds(r0, rows), pl.ds(c0 + 128 * i, 128)] += v.reshape(rows, 128)

    msgs = {}
    sides = [(half, sign, s) for half in (0, 1) for sign, s in ((1, 0), (-1, 1))]

    def far_send():
        for half, _, s in sides:
            encode(scores, 3 * CHUNK + half * BUNDLE + s * OWN, OWN, 0, D, far_out.at[half, s])
        for half, sign, s in sides:
            msgs["far", half, s] = send(far_out.at[half, s], far_in.at[half, s], **{second_axis[half]: sign})

    def near_send():
        for half, _, s in sides:
            encode(scores, near_rows(half, s, 1 - s), OWN, 0, D, near_out.at[half, s])
        for half, sign, s in sides:
            msgs["near", half, s] = send(near_out.at[half, s], near_in.at[half, s], **{second_axis[half]: sign})

    def far_wait():
        for half, _, s in sides:
            msgs["far", half, s].wait_recv()

    def rest_encode():
        for half, _, s in sides:
            row = near_rows(half, s, s)
            add_decoded(scores, row, OWN, 0, D, far_in.at[half, s])
            for u in (0, 1):
                encode(scores, row + (1 - u) * HALF, HALF, 0, D, rest_out.at[half, s, u])

    def rest_send():
        for u in (0, 1):
            for half, sign, s in sides:
                msgs["rest", half, s, u] = send(
                    rest_out.at[half, s, u], rest_in.at[half, s, u], **{second_axis[half]: sign}
                )

    def near_add():
        for half, _, s in sides:
            msgs["near", half, s].wait_recv()
        for half, _, s in sides:
            add_decoded(scores, half * BUNDLE + (1 - s) * OWN, OWN, 0, D, near_in.at[half, s])

    def rest_add(u):
        for half, _, s in sides:
            msgs["rest", half, s, u].wait_recv()
        for half, _, s in sides:
            add_decoded(scores, half * BUNDLE + s * OWN + (1 - u) * HALF, HALF, 0, D, rest_in.at[half, s, u])

    def last_send(*qs):
        for half in (0, 1):
            for q in qs:
                encode(scores, half * BUNDLE + q * HALF, HALF, 0, D, last_out.at[half, q - 1])
        for q in qs:
            for half in (0, 1):
                msgs["last", half, q] = send(
                    last_out.at[half, q - 1], last_in.at[half, q - 1], **{first_axis[half]: RING4[q]}
                )

    def query_out():
        for q in (1, 3, 2):
            for half in (0, 1):
                msgs["last", half, q].wait_recv()
            for half in (0, 1):
                add_decoded(scores, half * BUNDLE, HALF, 0, D, last_in.at[half, q - 1])
        for half in (0, 1):
            rows = pl.ds(half * BUNDLE, HALF)
            qg_out[pl.ds(half * HALF, HALF), :] = (scores[rows, pl.ds(0, D)] * GRAD_SCALE).astype(bf16)

    def z_far():
        for s in (0, 1):
            encode(term, 7 * BUNDLE + s * HALF, HALF, 0, D, z_far_out.at[s])
        for sign, s in ((1, 0), (-1, 1)):
            msgs["z", 4, s] = send(z_far_out.at[s], z_far_in.at[s], dz=sign)

    def z_near(k, part):
        rows = [AT8[sign * k] * BUNDLE + (s if part else 1 - s) * HALF for sign, s in ((1, 0), (-1, 1))]
        if k < 3:
            arrived = [(msgs["z", k + 1, s, part], z_in.at[k, s, part]) for s in (0, 1)]
        else:
            arrived = [(msgs["z", 4, s], z_far_in.at[s]) for s in (0, 1)] if part else []
        for message, _ in arrived:
            message.wait_recv()
        for row, (_, buf) in zip(rows, arrived):
            add_decoded(term, row, HALF, 0, D, buf)
        for s in (0, 1):
            encode(term, rows[s], HALF, 0, D, z_out.at[k - 1, s, part])
        for sign, s in ((1, 0), (-1, 1)):
            msgs["z", k, s, part] = send(z_out.at[k - 1, s, part], z_in.at[k - 1, s, part], dz=sign)

    def passage_out():
        for part in (0, 1):
            for s in (0, 1):
                msgs["z", 1, s, part].wait_recv()
            for s in (0, 1):
                add_decoded(term, (s if part else 1 - s) * HALF, HALF, 0, D, z_in.at[0, s, part])
        pg_out[...] = (term[pl.ds(0, OWN), :] * GRAD_SCALE).astype(bf16)

    loss_slot = [0]

    def total_along(value, axis, size):
        base = loss_slot[0]
        loss_slot[0] += size
        loss_out_buf[base] = value
        copies = [
            send(loss_out_buf.at[base], loss_in_buf.at[base + d], **{axis: d}) for d in range(1, size)
        ]

        def finish():
            out = value
            for d, m in enumerate(copies, 1):
                m.wait_recv()
                out = out + loss_in_buf[base + d]
            return out

        return finish

    for p in range(4):
        weigh(p, 3)
    passage_term(3)
    for k in range(3):
        weigh(3, k)
    sib_send(3)
    query_term(3)
    for p in range(3):
        weigh(p, 2)
    far_send()
    add_sibling(7)
    z_far()
    passage_term(2)
    for p in (1, 2):
        for k in (0, 1):
            weigh(p, k)
    sib_send(2)
    near_terms(0)
    for k in (0, 1):
        weigh(0, k)
    near_send()
    finish = total_along(share * (1.0 / 16.0) - 2.0 * positive[...], "dz", 8)
    add_sibling(5, 6)
    z_near(3, 0)
    z_near(3, 1)
    passage_term(1)
    sib_send(1)
    near_terms(1)
    finish = total_along(finish(), "dx", 4)
    far_wait()
    rest_encode()
    rest_send()
    add_sibling(3, 4)
    z_near(2, 0)
    passage_term(0)
    sib_send(0)
    finish = total_along(finish(), "dy", 4)
    z_near(2, 1)
    query_term(0)
    finish = total_along(finish(), "dc", 2)
    near_add()
    rest_add(0)
    last_send(3, 1)
    add_sibling(1, 2, 0)
    z_near(1, 0)
    rest_add(1)
    last_send(2)
    z_near(1, 1)
    total = finish()
    loss_out[...] = jnp.sum(jnp.sum(total, axis=1, keepdims=True), axis=0, keepdims=True) * (LN2 / (2.0 * PAIRS))
    query_out()
    passage_out()
    for copy in sent:
        copy.wait_send()


def on_device(queries, passages, pair):
    vmem = pl.BlockSpec(memory_space=pltpu.VMEM)
    anywhere = pl.BlockSpec(memory_space=pl.ANY)
    query_grad, passage_grad, loss = pl.pallas_call(
        kernel,
        out_shape=(
            pltpu.VMEM((OWN, D), bf16),
            pltpu.VMEM((OWN, D), bf16),
            jax.ShapeDtypeStruct((1, 1), f32),
        ),
        in_specs=[anywhere] * 3,
        out_specs=[vmem] * 3,
        scratch_shapes=[
            pltpu.VMEM((ROWS, D), bf16),
            pltpu.VMEM((ROWS, D), bf16),
            pltpu.VMEM((1, OWN), jnp.int32),
            pltpu.VMEM((ROWS, ROWS), f32),
            pltpu.VMEM((ROWS, ROWS), bf16),
            pltpu.VMEM((ROWS, 128), f32),
            pltpu.VMEM((ROWS, 128), f32),
            pltpu.VMEM((8, ROWS), f32),
            pltpu.VMEM((8, ROWS), f32),
            pltpu.VMEM((16, 16, 128), f32),
            pltpu.VMEM((16, 16, 128), f32),
            pltpu.VMEM((16, 128), f32),
            pltpu.VMEM((16, 128), f32),
            pltpu.VMEM((ROWS, 128), f32),
            pltpu.VMEM((ROWS, 128), f32),
            pltpu.VMEM((128, 128), f32),
            pltpu.VMEM((16, 128), f32),
            pltpu.VMEM((1, ROWS), f32),
            pltpu.VMEM((1, ROWS), f32),
            pltpu.VMEM((ROWS, D), f32),
            pltpu.VMEM((ROWS // 2, D), f32),
            pltpu.VMEM((2, 2, tiles(OWN, D), 16, 128), i16),
            pltpu.VMEM((2, 2, tiles(OWN, D), 16, 128), i16),
            pltpu.VMEM((2, 2, tiles(OWN, D), 16, 128), i16),
            pltpu.VMEM((2, 2, tiles(OWN, D), 16, 128), i16),
            pltpu.VMEM((2, 2, 2, tiles(HALF, D), 16, 128), i16),
            pltpu.VMEM((2, 2, 2, tiles(HALF, D), 16, 128), i16),
            pltpu.VMEM((2, 3, tiles(HALF, D), 16, 128), i16),
            pltpu.VMEM((2, 3, tiles(HALF, D), 16, 128), i16),
            pltpu.VMEM((2, tiles(HALF, D), 16, 128), i16),
            pltpu.VMEM((2, tiles(HALF, D), 16, 128), i16),
            pltpu.VMEM((3, 2, 2, tiles(HALF, D), 16, 128), i16),
            pltpu.VMEM((3, 2, 2, tiles(HALF, D), 16, 128), i16),
            pltpu.VMEM((18, 8, 128), f32),
            pltpu.VMEM((18, 8, 128), f32),
            pltpu.VMEM((8, 128), f32),
            pltpu.SemaphoreType.DMA((MESSAGES,)),
            pltpu.SemaphoreType.DMA((MESSAGES,)),
            pltpu.SemaphoreType.DMA((4,)),
        ],
        compiler_params=pltpu.CompilerParams(
            collective_id=0, has_side_effects=True, vmem_limit_bytes=60 * 1024 * 1024
        ),
    )(queries, passages, pair.reshape(1, OWN))
    return query_grad, passage_grad, loss.reshape(())


def solution(mesh):
    in_specs = (P(("loop", "grp"), None), P(("grp", "loop"), None), P(("loop", "grp")))
    out_specs = (P(("loop", "grp"), None), P(("grp", "loop"), None), P())
    return jax.shard_map(
        on_device, mesh=mesh, in_specs=in_specs, out_specs=out_specs, check_vma=False
    )
```

```python
import functools
import math

import jax
import jax.numpy as jnp
from jax import lax
from jax.experimental import pallas as pl
from jax.experimental.pallas import tpu as pltpu
from jax.sharding import PartitionSpec as P

MESH = pl.DeviceIdType.MESH
D = 1024
OWN = 96
HALF = 48
ROWS = 1536
BUNDLE = 192
CHUNK = 384
COLS = 512
PAIRS = 24576
TO_LOG2 = 50.0 * math.log2(math.e)
LN2 = math.log(2.0)
GRAD_SCALE = 25.0
LEVELS = 32000.0
SMALLEST = 1e-30
LOWEST = -1e38
RING4 = (0, 1, -1, 2)
RING8 = (0, 1, -1, 2, -2, 3, -3, 4)
AT4 = {0: 0, 1: 1, -1: 2, 2: 3}
AT8 = {0: 0, 1: 1, -1: 2, 2: 3, -2: 4, 3: 5, -3: 6, 4: 7}
MESSAGES = 144
f32 = jnp.float32
bf16 = jnp.bfloat16
i16 = jnp.int16


def tiles(rows, cols):
    return (rows // 16) * (cols // 128) + 1


def kernel(
    q_in, p_in, pair_in, qg_out, pg_out, loss_out,
    q_all, p_all, pair_own, scores, w,
    row_peak, row_sum, col_peak, col_sum,
    row_stats, col_stats, row_lse, pair_all, row_rep, pair_rep, order, col_lse, col_rep, col_index,
    term, sib, far_out, far_in, near_out, near_in, rest_out, rest_in, last_out, last_in,
    z_far_out, z_far_in, z_out, z_in, loss_out_buf, loss_in_buf, positive,
    send_sem, recv_sem, own_sem,
):
    loop = lax.axis_index("loop")
    grp = lax.axis_index("grp")
    core = lax.rem(grp, 2)
    x = lax.rem(lax.div(grp, 2), 4)
    y = lax.div(loop, 8) * 2 + lax.div(grp, 8)
    z = lax.rem(loop, 8)

    xs = [x] + [lax.rem(x + d, 4) for d in (1, 2, 3)]
    ys = [y] + [lax.rem(y + d, 4) for d in (1, 2, 3)]
    zs8 = [z] + [lax.rem(z + d, 8) for d in range(1, 8)]
    cores = [core, 1 - core]
    y_loop = [lax.div(v, 2) * 8 for v in ys]
    y_grp = [lax.rem(v, 2) * 8 for v in ys]

    def device(dx=0, dy=0, dz=0, dc=0):
        return {
            "loop": y_loop[dy % 4] + zs8[dz % 8],
            "grp": y_grp[dy % 4] + xs[dx % 4] * 2 + cores[dc],
        }

    def hops(d, size):
        return min(d, size - d)

    plane = [(dx, dy) for dx in range(4) for dy in range(4) if dx or dy]
    plane.sort(key=lambda d: -hops(d[0], 4) - hops(d[1], 4))
    column = [(dz, dc) for dz in range(8) for dc in range(2) if dz or dc]
    column.sort(key=lambda d: -hops(d[0], 8) * 2 - d[1])

    barrier = pltpu.get_barrier_semaphore()
    neighbours = [{"dx": 1}, {"dx": -1}, {"dy": 1}, {"dy": -1}, {"dz": 1}, {"dz": -1}, {"dc": 1}]
    neighbours += [{"dx": 2}, {"dy": 2}]
    for where in neighbours:
        pl.semaphore_signal(barrier, inc=1, device_id=device(**where), device_id_type=MESH)
    own = [
        pltpu.make_async_copy(src, dst, own_sem.at[k])
        for k, (src, dst) in enumerate(
            (
                (q_in.at[pl.ds(0, HALF), :], q_all.at[pl.ds(0, HALF), :]),
                (q_in.at[pl.ds(HALF, HALF), :], q_all.at[pl.ds(BUNDLE, HALF), :]),
                (p_in, p_all.at[pl.ds(0, OWN), :]),
                (pair_in, pair_own),
            )
        )
    ]
    for copy in own:
        copy.start()

    count = [0]
    sent = []

    def send(src, dst, **where):
        k = count[0]
        count[0] += 1
        copy = pltpu.make_async_remote_copy(
            src_ref=src, dst_ref=dst, send_sem=send_sem.at[k], recv_sem=recv_sem.at[k],
            device_id=device(**where), device_id_type=MESH,
        )
        copy.start()
        sent.append(copy)
        return copy

    def q_at(half, p, q):
        return q_all.at[pl.ds((2 * p + half) * BUNDLE + q * HALF, HALF), :]

    def p_at(pos, rel, h=None):
        start = pos * BUNDLE + rel * OWN
        if h is None:
            return p_all.at[pl.ds(start, OWN), :]
        return p_all.at[pl.ds(start + h * HALF, HALF), :]

    pl.semaphore_wait(barrier, len(neighbours))
    for copy in own:
        copy.wait()

    first_axis, second_axis = ("dx", "dy"), ("dy", "dx")
    zs, near1, far1, near2, far2, sibling = {}, {}, {}, {}, {}, {}

    def spread(half, q):
        for sign in (1, -1):
            near2[half, sign, q] = send(
                q_at(half, 0, q), q_at(half, AT4[-sign], q), **{second_axis[half]: sign}
            )

    def z_own(h):
        for sign in (1, -1):
            zs[sign, 1, h] = send(p_at(0, 0, h), p_at(AT8[-sign], 0, h), dz=sign)

    def z_pass(k, h):
        for sign in (1, -1):
            last = h != (0 if sign == 1 else 1)
            if k == 4 and last:
                continue
            zs[sign, k, h].wait_recv()
            if k < 3 or (k == 3 and not last):
                pos, to = AT8[-sign * k], AT8[-sign * (k + 1)] if k < 3 else 7
                zs[sign, k + 1, h] = send(p_at(pos, 0, h), p_at(to, 0, h), dz=sign)

    def to_sibling(*positions):
        for pos in positions:
            sibling[pos] = send(p_at(pos, 0), p_at(pos, 1), dc=1)

    def pass_far(q):
        for half in (0, 1):
            for sign in (1, -1):
                near2[half, sign, q].wait_recv()
                if (q < 2) == (sign == 1):
                    far2[half, q] = send(
                        q_at(half, AT4[-sign], q), q_at(half, 3, q), **{second_axis[half]: sign}
                    )

    for half in (0, 1):
        for sign in (1, -1):
            near1[half, sign] = send(q_at(half, 0, 0), q_at(half, 0, AT4[-sign]), **{first_axis[half]: sign})
    z_own(0)
    for half in (0, 1):
        far1[half] = send(q_at(half, 0, 0), q_at(half, 0, 3), **{first_axis[half]: 2})
    for half in (0, 1):
        spread(half, 0)
    z_own(1)
    to_sibling(0)
    row_peak[...] = jnp.full(row_peak.shape, LOWEST, f32)
    row_sum[...] = jnp.zeros(row_sum.shape, f32)
    col_peak[...] = jnp.full(col_peak.shape, LOWEST, f32)
    col_sum[...] = jnp.zeros(col_sum.shape, f32)
    slot = x * 4 + y
    col_slot = z * 2 + core
    row_stats[slot] = jnp.zeros((16, 128), f32)
    col_stats[col_slot] = jnp.zeros((16, 128), f32)
    for i in range(3):
        row_stats[slot, pl.ds(i, 1), pl.ds(OWN, 32)] = pair_own[:, 32 * i : 32 * (i + 1)].astype(f32)

    z_pass(1, 0)
    for half in (0, 1):
        for sign in (1, -1):
            near1[half, sign].wait_recv()
            spread(half, AT4[-sign])
    z_pass(1, 1)
    to_sibling(1, 2)
    pass_far(0)
    for half in (0, 1):
        far1[half].wait_recv()
        spread(half, 3)
    z_pass(2, 0)

    def block(p, start, width, chunks=1):
        height = chunks * CHUNK
        rows = pl.ds(p * CHUNK, height)
        cols = pl.ds(start, width)
        s = lax.dot_general(
            q_all[rows, :], p_all[cols, :], (((1,), (1,)), ((), ())), preferred_element_type=f32
        ) * TO_LOG2
        scores[rows, cols] = s
        parts = [s[:, 128 * i : 128 * (i + 1)] for i in range(width // 128)]
        old = row_peak[rows, :]
        peak = functools.reduce(jnp.maximum, parts, old)
        total = row_sum[rows, :] * jnp.exp2(old - peak)
        for part in parts:
            total += jnp.exp2(part - peak)
        row_peak[rows, :] = peak
        row_sum[rows, :] = total
        s3 = s.reshape(height // 8, 8, width)
        old = col_peak[:, cols]
        peak = jnp.maximum(old, jnp.max(s3, axis=0))
        col_sum[:, cols] = col_sum[:, cols] * jnp.exp2(old - peak) + jnp.sum(jnp.exp2(s3 - peak[None]), axis=0)
        col_peak[:, cols] = peak

    for pos in (0, 1, 2):
        sibling[pos].wait_recv()
    block(0, 0, 512)
    pass_far(1)
    z_pass(2, 1)
    to_sibling(3, 4)
    pass_far(2)
    z_pass(3, 0)
    pass_far(3)
    block(1, 0, 512)
    z_pass(3, 1)
    to_sibling(5, 6)
    block(2, 0, 512)
    for pos in (3, 4, 5, 6):
        sibling[pos].wait_recv()
    block(0, 512, 512)
    z_pass(4, 0)
    z_pass(4, 1)
    to_sibling(7)
    block(1, 512, 512)
    block(2, 512, 512)
    for p in range(3):
        block(p, 1024, 256)
    for half in (0, 1):
        for q in range(4):
            far2[half, q].wait_recv()
    block(3, 0, 1280)
    sibling[7].wait_recv()

    def piece(half, p, q):
        dx, dy = (RING4[q], RING4[p]) if half == 0 else (RING4[p], RING4[q])
        return xs[dx % 4] * 4 + ys[dy % 4]

    def owner(pos, rel):
        return zs8[RING8[pos] % 8] * 2 + cores[rel]

    def finish_rows(p):
        rows = pl.ds(p * CHUNK, CHUNK)
        lanes = row_peak[rows, :].T
        peak = jnp.max(lanes, axis=0, keepdims=True)
        total = jnp.sum(row_sum[rows, :].T * jnp.exp2(lanes - peak), axis=0, keepdims=True)
        lse = peak + jnp.log(total) * (1.0 / LN2)
        for half in (0, 1):
            for q in range(4):
                start = half * BUNDLE + q * HALF
                row_stats[slot, pl.ds(piece(half, p, q), 1), pl.ds(half * HALF, HALF)] = lse[:, start : start + HALF]

    block(0, 1280, 256, 4)
    for p in range(3):
        finish_rows(p)
    peak = jnp.max(col_peak[...], axis=0, keepdims=True)
    total = jnp.sum(col_sum[...] * jnp.exp2(col_peak[...] - peak), axis=0, keepdims=True)
    lse = peak + jnp.log(total) * (1.0 / LN2)
    for pos in range(8):
        for rel in (0, 1):
            start = pos * BUNDLE + rel * OWN
            col_stats[col_slot, pl.ds(owner(pos, rel), 1), pl.ds(0, OWN)] = lse[:, start : start + OWN]
    finish_rows(3)
    row_msgs, col_msgs = [], []
    for (dx, dy), (dz, dc) in zip(plane, column, strict=True):
        row_msgs.append(send(row_stats.at[slot], row_stats.at[slot], dx=dx, dy=dy))
        col_msgs.append(send(col_stats.at[col_slot], col_stats.at[col_slot], dz=dz, dc=dc))

    j = lax.broadcasted_iota(jnp.int32, (1, ROWS), 1)
    part = lax.shift_right_logical(j * 683, 16)
    within = j - part * OWN
    pos = lax.shift_right_logical(part, 1)
    away = lax.shift_right_logical(pos + 1, 1)
    away = jnp.where((pos & 1) == 1, away, -away)
    z2 = (z + away + 8) & 7
    c2 = (core + part) & 1
    first = (lax.div(grp, 2) * 2 + c2) * 16 + lax.div(loop, 8) * 8 + z2
    col_index[...] = (first * OWN + within).astype(f32)

    for m in row_msgs:
        m.wait_recv()
    stats = row_stats[...]
    lane = lax.broadcasted_iota(jnp.int32, (16, 128), 1)
    peak = jnp.max(stats, axis=0)
    lse = peak + jnp.log(jnp.sum(jnp.exp2(stats - peak[None]), axis=0)) * (1.0 / LN2)
    row_lse[...] = lse
    share = jnp.sum(jnp.where(lane < OWN, lse, 0.0).reshape(2, 8, 128), axis=0)
    for i in range(3):
        pair_all[:, pl.ds(32 * i, 32)] = stats[:, i, OWN:128]
    order[pl.ds(64, 64), :] = jnp.zeros((64, 128), f32)
    for b in range(8):
        p, half = b // 2, b % 2
        for q in range(4):
            at = piece(half, p, q)
            order[pl.ds(4 * b + q, 1), :] = row_lse[pl.ds(at, 1), :]
            order[pl.ds(32 + 4 * b + q, 1), :] = pair_all[pl.ds(at, 1), :]
    turned = order[...].T
    for b in range(8):
        half = b % 2
        for q in range(4):
            n = 4 * b + q
            rows = pl.ds(n * HALF, HALF)
            mine = turned[half * HALF : (half + 1) * HALF, :]
            row_rep[rows, :] = jnp.broadcast_to(mine[:, n : n + 1], (HALF, 128))
            pair_rep[rows, :] = jnp.broadcast_to(mine[:, 32 + n : 33 + n], (HALF, 128))

    for m in col_msgs:
        m.wait_recv()
    stats = col_stats[...]
    peak = jnp.max(stats, axis=0)
    lse = peak + jnp.log(jnp.sum(jnp.exp2(stats - peak[None]), axis=0)) * (1.0 / LN2)
    col_lse[...] = lse
    share = share + jnp.sum(jnp.where(lane < OWN, lse, 0.0).reshape(2, 8, 128), axis=0)
    col_rep[...] = jnp.concatenate(
        [col_lse[pl.ds(owner(pos, rel), 1), :][:, 0:OWN] for pos in range(8) for rel in (0, 1)], axis=1
    )

    positive[...] = jnp.zeros((8, 128), f32)

    def weigh(p, k):
        rows, cols = pl.ds(p * CHUNK, CHUNK), pl.ds(k * CHUNK, CHUNK)
        s = scores[rows, cols]
        hit = jnp.concatenate([pair_rep[rows, :]] * 3, axis=1) == col_index[:, cols]
        weight = (
            jnp.exp2(s - jnp.concatenate([row_rep[rows, :]] * 3, axis=1))
            + jnp.exp2(s - col_rep[:, cols])
            - jnp.where(hit, 2.0, 0.0)
        )
        found = jnp.sum(jnp.where(hit, s, 0.0).reshape(CHUNK // 8, 8, CHUNK), axis=0)
        positive[...] += found[:, 0:128] + found[:, 128:256] + found[:, 256:384]
        w[rows, cols] = weight.astype(bf16)

    def query_term(p):
        rows = pl.ds(p * CHUNK, CHUNK)
        scores[rows, pl.ds(0, D)] = jnp.dot(w[rows, :], p_all[...], preferred_element_type=f32)

    def near_rows(half, s, side):
        return (1 + s) * CHUNK + half * BUNDLE + side * OWN

    def near_terms(part):
        starts = [near_rows(half, s, s if part else 1 - s) for half in (0, 1) for s in (0, 1)]
        rows = jnp.concatenate([w[pl.ds(start, OWN), :] for start in starts], axis=0)
        out = jnp.dot(rows, p_all[...], preferred_element_type=f32)
        for i, start in enumerate(starts):
            scores[pl.ds(start, OWN), pl.ds(0, D)] = out[i * OWN : (i + 1) * OWN, :]

    sib_msgs = {}

    def passage_term(k):
        rows = pl.ds(k * CHUNK, CHUNK)
        term[rows, :] = lax.dot_general(
            w[:, rows], q_all[...], (((0,), (0,)), ((), ())), preferred_element_type=f32
        )

    def sib_send(k):
        for pos in (2 * k + 1, 2 * k):
            sib_msgs[pos] = send(
                term.at[pl.ds(pos * BUNDLE + OWN, OWN), :], sib.at[pl.ds(pos * OWN, OWN), :], dc=1
            )

    def add_sibling(*positions):
        for pos in positions:
            sib_msgs[pos].wait_recv()
        for pos in positions:
            term[pl.ds(pos * BUNDLE, OWN), :] += sib[pl.ds(pos * OWN, OWN), :]

    def encode(ref, r0, rows, c0, cols, buf):
        peak = functools.reduce(
            jnp.maximum,
            [
                jnp.max(jnp.abs(ref[pl.ds(r0, rows), pl.ds(c0 + 128 * i, 128)]).reshape(rows // 8, 8, 128), axis=0)
                for i in range(cols // 128)
            ],
        )
        power = jnp.floor(jnp.log(jnp.maximum(peak, SMALLEST)) * (1.0 / LN2)) + 1.0
        factor = (jnp.exp2(-power) * LEVELS)[None]
        n = rows // 16
        for i in range(cols // 128):
            v = ref[pl.ds(r0, rows), pl.ds(c0 + 128 * i, 128)].reshape(rows // 8, 8, 128) * factor
            buf[pl.ds(i * n, n)] = jnp.round(v).astype(jnp.int32).reshape(n, 16, 128).astype(i16)
        both = jnp.concatenate([power, power], axis=0).astype(jnp.int32)
        buf[pl.ds(n * (cols // 128), 1)] = both.astype(i16)[None]

    def add_decoded(ref, r0, rows, c0, cols, buf):
        n = rows // 16
        power = buf[n * (cols // 128)].astype(jnp.int32).astype(f32)[0:8]
        factor = (jnp.exp2(power) * (1.0 / LEVELS))[None]
        for i in range(cols // 128):
            v = buf[pl.ds(i * n, n)].astype(jnp.int32).astype(f32).reshape(rows // 8, 8, 128) * factor
            ref[pl.ds(r0, rows), pl.ds(c0 + 128 * i, 128)] += v.reshape(rows, 128)

    msgs = {}
    sides = [(half, sign, s) for half in (0, 1) for sign, s in ((1, 0), (-1, 1))]

    def far_send():
        for half, _, s in sides:
            encode(scores, 3 * CHUNK + half * BUNDLE + s * OWN, OWN, 0, D, far_out.at[half, s])
        for half, sign, s in sides:
            msgs["far", half, s] = send(far_out.at[half, s], far_in.at[half, s], **{second_axis[half]: sign})

    def near_send():
        for half, _, s in sides:
            encode(scores, near_rows(half, s, 1 - s), OWN, 0, D, near_out.at[half, s])
        for half, sign, s in sides:
            msgs["near", half, s] = send(near_out.at[half, s], near_in.at[half, s], **{second_axis[half]: sign})

    def far_wait():
        for half, _, s in sides:
            msgs["far", half, s].wait_recv()

    def rest_encode():
        for half, _, s in sides:
            row = near_rows(half, s, s)
            add_decoded(scores, row, OWN, 0, D, far_in.at[half, s])
            for u in (0, 1):
                encode(scores, row + (1 - u) * HALF, HALF, 0, D, rest_out.at[half, s, u])

    def rest_send():
        for u in (0, 1):
            for half, sign, s in sides:
                msgs["rest", half, s, u] = send(
                    rest_out.at[half, s, u], rest_in.at[half, s, u], **{second_axis[half]: sign}
                )

    def near_add():
        for half, _, s in sides:
            msgs["near", half, s].wait_recv()
        for half, _, s in sides:
            add_decoded(scores, half * BUNDLE + (1 - s) * OWN, OWN, 0, D, near_in.at[half, s])

    def rest_add(u):
        for half, _, s in sides:
            msgs["rest", half, s, u].wait_recv()
        for half, _, s in sides:
            add_decoded(scores, half * BUNDLE + s * OWN + (1 - u) * HALF, HALF, 0, D, rest_in.at[half, s, u])

    def last_send(*qs):
        for half in (0, 1):
            for q in qs:
                encode(scores, half * BUNDLE + q * HALF, HALF, 0, D, last_out.at[half, q - 1])
        for q in qs:
            for half in (0, 1):
                msgs["last", half, q] = send(
                    last_out.at[half, q - 1], last_in.at[half, q - 1], **{first_axis[half]: RING4[q]}
                )

    def query_out():
        for q in (1, 3, 2):
            for half in (0, 1):
                msgs["last", half, q].wait_recv()
            for half in (0, 1):
                add_decoded(scores, half * BUNDLE, HALF, 0, D, last_in.at[half, q - 1])
        for half in (0, 1):
            rows = pl.ds(half * BUNDLE, HALF)
            qg_out[pl.ds(half * HALF, HALF), :] = (scores[rows, pl.ds(0, D)] * GRAD_SCALE).astype(bf16)

    def z_far():
        for s in (0, 1):
            encode(term, 7 * BUNDLE + s * HALF, HALF, 0, D, z_far_out.at[s])
        for sign, s in ((1, 0), (-1, 1)):
            msgs["z", 4, s] = send(z_far_out.at[s], z_far_in.at[s], dz=sign)

    def z_near(k, part):
        rows = [AT8[sign * k] * BUNDLE + (s if part else 1 - s) * HALF for sign, s in ((1, 0), (-1, 1))]
        if k < 3:
            arrived = [(msgs["z", k + 1, s, part], z_in.at[k, s, part]) for s in (0, 1)]
        else:
            arrived = [(msgs["z", 4, s], z_far_in.at[s]) for s in (0, 1)] if part else []
        for message, _ in arrived:
            message.wait_recv()
        for row, (_, buf) in zip(rows, arrived):
            add_decoded(term, row, HALF, 0, D, buf)
        for s in (0, 1):
            encode(term, rows[s], HALF, 0, D, z_out.at[k - 1, s, part])
        for sign, s in ((1, 0), (-1, 1)):
            msgs["z", k, s, part] = send(z_out.at[k - 1, s, part], z_in.at[k - 1, s, part], dz=sign)

    def passage_out():
        for part in (0, 1):
            for s in (0, 1):
                msgs["z", 1, s, part].wait_recv()
            for s in (0, 1):
                add_decoded(term, (s if part else 1 - s) * HALF, HALF, 0, D, z_in.at[0, s, part])
        pg_out[...] = (term[pl.ds(0, OWN), :] * GRAD_SCALE).astype(bf16)

    loss_slot = [0]

    def total_along(value, axis, size):
        base = loss_slot[0]
        loss_slot[0] += size
        loss_out_buf[base] = value
        copies = [
            send(loss_out_buf.at[base], loss_in_buf.at[base + d], **{axis: d}) for d in range(1, size)
        ]

        def finish():
            out = value
            for d, m in enumerate(copies, 1):
                m.wait_recv()
                out = out + loss_in_buf[base + d]
            return out

        return finish

    for p in range(4):
        weigh(p, 3)
    passage_term(3)
    for k in range(3):
        weigh(3, k)
    sib_send(3)
    query_term(3)
    for p in range(3):
        weigh(p, 2)
    far_send()
    add_sibling(7)
    z_far()
    passage_term(2)
    for p in (1, 2):
        for k in (0, 1):
            weigh(p, k)
    sib_send(2)
    near_terms(0)
    for k in (0, 1):
        weigh(0, k)
    near_send()
    finish = total_along(share * (1.0 / 16.0) - 2.0 * positive[...], "dz", 8)
    add_sibling(5, 6)
    z_near(3, 0)
    z_near(3, 1)
    passage_term(1)
    sib_send(1)
    near_terms(1)
    finish = total_along(finish(), "dx", 4)
    far_wait()
    rest_encode()
    rest_send()
    add_sibling(3, 4)
    z_near(2, 0)
    passage_term(0)
    sib_send(0)
    finish = total_along(finish(), "dy", 4)
    z_near(2, 1)
    query_term(0)
    finish = total_along(finish(), "dc", 2)
    near_add()
    rest_add(0)
    last_send(3, 1)
    add_sibling(1, 2, 0)
    z_near(1, 0)
    rest_add(1)
    last_send(2)
    z_near(1, 1)
    total = finish()
    loss_out[...] = jnp.sum(jnp.sum(total, axis=1, keepdims=True), axis=0, keepdims=True) * (LN2 / (2.0 * PAIRS))
    query_out()
    passage_out()
    for copy in sent:
        copy.wait_send()


def on_device(queries, passages, pair):
    vmem = pl.BlockSpec(memory_space=pltpu.VMEM)
    anywhere = pl.BlockSpec(memory_space=pl.ANY)
    query_grad, passage_grad, loss = pl.pallas_call(
        kernel,
        out_shape=(
            pltpu.VMEM((OWN, D), bf16),
            pltpu.VMEM((OWN, D), bf16),
            jax.ShapeDtypeStruct((1, 1), f32),
        ),
        in_specs=[anywhere] * 3,
        out_specs=[vmem] * 3,
        scratch_shapes=[
            pltpu.VMEM((ROWS, D), bf16),
            pltpu.VMEM((ROWS, D), bf16),
            pltpu.VMEM((1, OWN), jnp.int32),
            pltpu.VMEM((ROWS, ROWS), f32),
            pltpu.VMEM((ROWS, ROWS), bf16),
            pltpu.VMEM((ROWS, 128), f32),
            pltpu.VMEM((ROWS, 128), f32),
            pltpu.VMEM((8, ROWS), f32),
            pltpu.VMEM((8, ROWS), f32),
            pltpu.VMEM((16, 16, 128), f32),
            pltpu.VMEM((16, 16, 128), f32),
            pltpu.VMEM((16, 128), f32),
            pltpu.VMEM((16, 128), f32),
            pltpu.VMEM((ROWS, 128), f32),
            pltpu.VMEM((ROWS, 128), f32),
            pltpu.VMEM((128, 128), f32),
            pltpu.VMEM((16, 128), f32),
            pltpu.VMEM((1, ROWS), f32),
            pltpu.VMEM((1, ROWS), f32),
            pltpu.VMEM((ROWS, D), f32),
            pltpu.VMEM((ROWS // 2, D), f32),
            pltpu.VMEM((2, 2, tiles(OWN, D), 16, 128), i16),
            pltpu.VMEM((2, 2, tiles(OWN, D), 16, 128), i16),
            pltpu.VMEM((2, 2, tiles(OWN, D), 16, 128), i16),
            pltpu.VMEM((2, 2, tiles(OWN, D), 16, 128), i16),
            pltpu.VMEM((2, 2, 2, tiles(HALF, D), 16, 128), i16),
            pltpu.VMEM((2, 2, 2, tiles(HALF, D), 16, 128), i16),
            pltpu.VMEM((2, 3, tiles(HALF, D), 16, 128), i16),
            pltpu.VMEM((2, 3, tiles(HALF, D), 16, 128), i16),
            pltpu.VMEM((2, tiles(HALF, D), 16, 128), i16),
            pltpu.VMEM((2, tiles(HALF, D), 16, 128), i16),
            pltpu.VMEM((3, 2, 2, tiles(HALF, D), 16, 128), i16),
            pltpu.VMEM((3, 2, 2, tiles(HALF, D), 16, 128), i16),
            pltpu.VMEM((18, 8, 128), f32),
            pltpu.VMEM((18, 8, 128), f32),
            pltpu.VMEM((8, 128), f32),
            pltpu.SemaphoreType.DMA((MESSAGES,)),
            pltpu.SemaphoreType.DMA((MESSAGES,)),
            pltpu.SemaphoreType.DMA((4,)),
        ],
        compiler_params=pltpu.CompilerParams(
            collective_id=0, has_side_effects=True, vmem_limit_bytes=60 * 1024 * 1024
        ),
    )(queries, passages, pair.reshape(1, OWN))
    return query_grad, passage_grad, loss.reshape(())


def solution(mesh):
    in_specs = (P(("loop", "grp"), None), P(("grp", "loop"), None), P(("loop", "grp")))
    out_specs = (P(("loop", "grp"), None), P(("grp", "loop"), None), P())
    return jax.shard_map(
        on_device, mesh=mesh, in_specs=in_specs, out_specs=out_specs, check_vma=False
    )
```
